256 devices in a mesh: az: 16 (over z, x_hi), rad: 2 (over core), ax: 8 (over y, x_lo).
Axes of the slice: x: 4 (x_hi: 2, x_lo: 2; x = x_hi * 2 + x_lo), y: 4, z: 8, core: 2. Of those that a mesh axis runs over, the one named last changes fastest.
Arguments:
- velocity: float32 [3, 128, 128, 1024], P(None, 'az', 'rad', 'ax'), may hold values from -6 to 6
- strain_rate: float32 [6, 128, 128, 1024], P(None, 'az', 'rad', 'ax'), may hold values from -6 to 6
- lm_average: float32 [128, 128, 1024], P('az', 'rad', 'ax'), may hold values from -8 to 8
- mm_average: float32 [128, 128, 1024], P('az', 'rad', 'ax'), may hold values from 1 to 20
- source_owner: int32 [128, 128, 8], P('az', 'rad', 'ax'), may hold values from 0 to 255, as said below
- source_block: int32 [128, 128, 8], P('az', 'rad', 'ax'), may hold values from 0 to 511
- offset_cells: int32 [128, 128, 8], P('az', 'rad', 'ax'), may hold values from 0 to 7
- fraction: float32 [128, 128, 8], P('az', 'rad', 'ax'), may hold values from 0 to 1
- query_count: int32 [256], replicated, may hold values from 64 to 512, as said below
Outputs:
- lm_updated: float32 [128, 128, 1024], P('az', 'rad', 'ax')
- mm_updated: float32 [128, 128, 1024], P('az', 'rad', 'ax')
- eddy_viscosity: float32 [128, 128, 1024], P('az', 'rad', 'ax')
The draws below stay inside these ranges and needn't reach their ends.
Inputs may be any that keep to these rules, and one draw needn't show every extreme that they name: `source_owner`: each block's source owner is the querying device itself, the device one az index lower or higher (around the loop of az), or the device whose rad index differs in the lowest bit; it has the querying device's ax index. Among the live blocks of one device at most 128 name any one owner, and a device with all 512 blocks live names each of the four exactly 128 times. `query_count`: some device has all 512 blocks live.
All inputs are finite; a program needn't handle non-finite values.
Results may differ from the reference program's by a relative error of at most 0.0012.
Values sent between devices are 32-bit elements; how exact they have to be, the bound alone decides.
A program may use at most 128 MiB of HBM per device.

```python
import math
import jax
import jax.numpy as jnp
from jax import lax

CA = 8
CR = 64
KB = 1
QB = 512
CAP = 128
NA = 128
NR = 128
NX = 1024
NXB = 8
DEVS = 256
N_RAD = 2
N_AX = 8


def draw_source_owner(key, part):
    n_az = NA // CA
    n_rad = NR // CR
    n_ax = NXB // KB
    keys = jax.random.split(jax.random.fold_in(key, 11), DEVS)
    orders = jax.vmap(lambda single: jax.random.permutation(single, QB))(keys)
    direction_table = (orders // CAP).astype(jnp.int32)
    glob_az = jnp.broadcast_to(jnp.arange(NA, dtype=jnp.int32)[:, None, None], (NA, NR, NXB))
    glob_rad = jnp.broadcast_to(jnp.arange(NR, dtype=jnp.int32)[None, :, None], (NA, NR, NXB))
    glob_ax = jnp.broadcast_to(jnp.arange(NXB, dtype=jnp.int32)[None, None, :], (NA, NR, NXB))
    index_az = glob_az // CA
    index_rad = glob_rad // CR
    index_ax = glob_ax // KB
    device = index_az * (n_rad * n_ax) + index_rad * n_ax + index_ax
    local_index = (glob_az % CA * CR + glob_rad % CR) * KB + glob_ax % KB
    direction = direction_table[device, local_index]
    target_az = jnp.where(direction == 1, jnp.remainder(index_az - 1, n_az), jnp.where(direction == 2, jnp.remainder(index_az + 1, n_az), index_az))
    target_rad = jnp.where(direction == 3, index_rad + 1 - 2 * (index_rad % 2), index_rad)
    return (target_az * (n_rad * n_ax) + target_rad * n_ax + index_ax).astype(jnp.int32)


def draw_query_count(key, part):
    key_base, key_hot, key_pick = jax.random.split(jax.random.fold_in(key, 23), 3)
    base = jax.random.randint(key_base, (DEVS,), QB // 8, QB // 2 + 1)
    hot = jax.random.randint(key_hot, (DEVS,), 0, 8) == 0
    chosen = jax.random.randint(key_pick, (), 0, DEVS)
    hot = hot | (jnp.arange(DEVS, dtype=jnp.int32) == chosen)
    return jnp.where(hot, QB, base).astype(jnp.int32)


def place_ends(entries, rng, low, high):
    longest = entries.shape.index(max(entries.shape))
    spots = []
    for shift in (0, 1):
        where = [jax.random.randint(jax.random.fold_in(rng, axis), (), 0, length) for axis, length in enumerate(entries.shape)]
        where[longest] = (where[longest] + shift) % entries.shape[longest]
        spots.append(tuple(where))
    return entries.at[spots[0]].set(low).at[spots[1]].set(high)


def block_scale(own_key, extent, shards, least, high):
    gain, own = 1.0, jax.random.fold_in(own_key, 6)
    for position, shards_of in shards:
        steps = jnp.exp(jax.random.uniform(jax.random.fold_in(own, position), (shards_of,), jnp.float32, least / len(shards), high / len(shards)))
        gain = gain * jnp.repeat(steps, extent[position] // shards_of).reshape([-1 if axis == position else 1 for axis in range(len(extent))])
    return gain


def normal_values(own_key, dims, width, most, cuts=(), kind=jnp.bfloat16):
    result = width * jax.random.normal(own_key, dims, jnp.float32)
    if cuts:
        result = result * block_scale(own_key, dims, cuts, -0.22, 0.18)
    return jnp.clip(result, -most, most).astype(kind)


def setup_inputs(seed: int = 0) -> dict:
    seeds = jax.random.split(jax.random.key(seed), 10)
    velocity = normal_values(seeds[0], (3, NA, NR, NX), 1.0, 6.0, ((1, 16), (2, 2), (3, 8)), jnp.float32)
    strain_rate = normal_values(seeds[1], (6, NA, NR, NX), 1.0, 6.0, ((1, 16), (2, 2), (3, 8)), jnp.float32)
    lm_average = normal_values(seeds[2], (NA, NR, NX), 2.0, 8.0, ((0, 16), (1, 2), (2, 8)), jnp.float32)
    mm_average = jnp.clip(jnp.exp(math.log(20.0) - 2.9957323 * jax.random.uniform(seeds[3], (NA, NR, NX), jnp.float32) ** block_scale(seeds[3], (NA, NR, NX), ((0, 16), (1, 2), (2, 8)), -0.2, 0.2)), 1.0, 20.0)
    source_owner = draw_source_owner(jax.random.fold_in(seeds[9], 71), 0)
    source_block = place_ends(jax.random.randint(seeds[5], (NA, NR, NXB), 0, QB), jax.random.fold_in(seeds[5], 1), 0, QB - 1).astype(jnp.int32)
    offset_cells = place_ends(jax.random.randint(seeds[6], (NA, NR, NXB), 0, 8), jax.random.fold_in(seeds[6], 1), 0, 7).astype(jnp.int32)
    fraction = jnp.clip(1.0 * jax.random.uniform(seeds[7], (NA, NR, NXB), jnp.float32) ** block_scale(seeds[7], (NA, NR, NXB), ((0, 16), (1, 2), (2, 8)), -0.2, 0.2), 0.0, 1.0)
    query_count = draw_query_count(jax.random.fold_in(seeds[9], 71), 0)
    return {"velocity": velocity, "strain_rate": strain_rate, "lm_average": lm_average, "mm_average": mm_average, "source_owner": source_owner, "source_block": source_block, "offset_cells": offset_cells, "fraction": fraction, "query_count": query_count}


pair_list = ((0, 0), (1, 1), (2, 2), (0, 1), (0, 2), (1, 2))
delta_sq = 0.25
relax_rate = 0.5

def strain_norm(strain):
    normal = strain[0] * strain[0] + strain[1] * strain[1] + strain[2] * strain[2]
    shearing = strain[3] * strain[3] + strain[4] * strain[4] + strain[5] * strain[5]
    return jnp.sqrt(2.0 * normal + 4.0 * shearing)

def products(velocity, strain, magnitude):
    fields = [velocity[0], velocity[1], velocity[2]]
    fields += [velocity[left_comp] * velocity[right_comp] for left_comp, right_comp in pair_list]
    fields += [strain[channel] for channel in range(6)]
    fields += [magnitude * strain[channel] for channel in range(6)]
    return fields

def contract(filtered):
    magnitude = strain_norm([filtered[9 + channel] for channel in range(6)])
    lm_sum = 0.0
    mm_sum = 0.0
    for channel, (left_comp, right_comp) in enumerate(pair_list):
        weight = 1.0 if channel < 3 else 2.0
        leonard = filtered[3 + channel] - filtered[left_comp] * filtered[right_comp]
        model_term = 2.0 * delta_sq * (filtered[15 + channel] - 4.0 * magnitude * filtered[9 + channel])
        lm_sum = lm_sum + weight * leonard * model_term
        mm_sum = mm_sum + weight * model_term * model_term
    return (lm_sum, mm_sum)

def smooth(values, axis_dim):
    interior = values.shape[axis_dim] - 2
    before = lax.slice_in_dim(values, 0, interior, axis=axis_dim)
    middle = lax.slice_in_dim(values, 1, interior + 1, axis=axis_dim)
    behind = lax.slice_in_dim(values, 2, interior + 2, axis=axis_dim)
    return 0.25 * before + 0.5 * middle + 0.25 * behind

def interpolate(line_values, offsets, fraction):
    positions = jnp.arange(128, dtype=jnp.int32)
    anchor = positions - offsets[..., None]
    left_cell = jnp.broadcast_to(jnp.clip(anchor, 0, 127)[None], line_values.shape)
    right_cell = jnp.broadcast_to(jnp.clip(anchor + 1, 0, 127)[None], line_values.shape)
    weight = fraction[None, ..., None]
    return (1.0 - weight) * jnp.take_along_axis(line_values, left_cell, axis=-1) + weight * jnp.take_along_axis(line_values, right_cell, axis=-1)

def relax(lm_here, mm_here, upstream_lm, upstream_mm, magnitude):
    rate_ratio = relax_rate * jnp.power(jnp.maximum(upstream_lm, 0.0) * upstream_mm, 0.125)
    weight = rate_ratio / (1.0 + rate_ratio)
    lm_new = jnp.maximum(weight * lm_here + (1.0 - weight) * upstream_lm, 0.0)
    mm_new = weight * mm_here + (1.0 - weight) * upstream_mm
    return (lm_new, mm_new, delta_sq * lm_new / mm_new * magnitude)

def smooth_global(values):
    values = smooth(jnp.pad(values, ((1, 1), (0, 0), (0, 0)), mode='wrap'), 0)
    values = smooth(jnp.pad(values, ((0, 0), (1, 1), (0, 0))), 1)
    return smooth(jnp.pad(values, ((0, 0), (0, 0), (1, 1))), 2)

def reference(velocity, strain_rate, lm_average, mm_average, source_owner, source_block, offset_cells, fraction, query_count):
    magnitude = strain_norm(strain_rate)
    fields = products(velocity, strain_rate, magnitude)
    filtered = [smooth_global(values) for values in fields]
    lm_here, mm_here = contract(filtered)
    blocks_axial = NX // 128
    block_table = jnp.stack([lm_average, mm_average]).reshape(2, NA, NR, blocks_axial, 128)
    owner_az = source_owner // (N_RAD * N_AX)
    owner_rad = source_owner // N_AX % N_RAD
    owner_ax = source_owner % N_AX
    local_az = source_block // (CR * KB)
    local_rad = source_block // KB % CR
    local_ax = source_block % KB
    picked = block_table[:, owner_az * CA + local_az, owner_rad * CR + local_rad, owner_ax * KB + local_ax, :]
    glob_az = jnp.arange(NA, dtype=jnp.int32)[:, None, None]
    glob_rad = jnp.arange(NR, dtype=jnp.int32)[None, :, None]
    glob_ax = jnp.arange(blocks_axial, dtype=jnp.int32)[None, None, :]
    device = glob_az // CA * (N_RAD * N_AX) + glob_rad // CR * N_AX + glob_ax // KB
    local_index = (glob_az % CA * CR + glob_rad % CR) * KB + glob_ax % KB
    active = local_index < query_count[device]
    line_values = jnp.where(active[None, ..., None], picked, block_table)
    upstream = interpolate(line_values, offset_cells, fraction).reshape(2, NA, NR, NX)
    lm_new, mm_new, eddy = relax(lm_here, mm_here, upstream[0], upstream[1], magnitude)
    return (lm_new, mm_new, eddy)
```

```python
import jax
import jax.numpy as jnp
from jax import lax
from jax.experimental import pallas as pl
from jax.experimental.pallas import tpu as pltpu
from jax.sharding import PartitionSpec as P

MESH = pl.DeviceIdType.MESH
pair_list = ((0, 0), (1, 1), (2, 2), (0, 1), (0, 2), (1, 2))
CA, CR, CX = 8, 64, 128
NCH = 21
LINES = CA * CR
CAP = LINES // 4
GROUPS = CR // 8
f32 = jnp.float32
VMEM_LIMIT = 48000 * 2**10


def strain_norm(s):
    normal = s[0] * s[0] + s[1] * s[1] + s[2] * s[2]
    shearing = s[3] * s[3] + s[4] * s[4] + s[5] * s[5]
    return jnp.sqrt(2.0 * normal + 4.0 * shearing)


def products(raw):
    vel, strain = raw[:3], raw[3:]
    magnitude = strain_norm(strain)
    fields = list(vel)
    fields += [vel[i] * vel[j] for i, j in pair_list]
    fields += strain
    fields += [magnitude * s for s in strain]
    return fields, magnitude


def contract(filtered):
    strain = [filtered[9 + c] for c in range(6)]
    four_norm = 4.0 * strain_norm(strain)
    sums = []
    for channels in ((0, 1, 2), (3, 4, 5)):
        lm = mm = None
        for c in channels:
            i, j = pair_list[c]
            leonard = filtered[3 + c] - filtered[i] * filtered[j]
            model = filtered[15 + c] - four_norm * strain[c]
            lm = leonard * model if lm is None else lm + leonard * model
            mm = model * model if mm is None else mm + model * model
        sums.append((lm, mm))
    (lm_a, mm_a), (lm_b, mm_b) = sums
    return 0.5 * lm_a + lm_b, 0.25 * mm_a + 0.5 * mm_b


def exchange_kernel(
    vel, strain, lm_avg, mm_avg, owner, block, offset, frac, count,
    lines, lm_here, mm_here, mag, columns_out,
    raw, cols, col_send, halo_prod, ax_done, az_done, row_send, row_recv, rad_done,
    own, table, reply, ask, asked_vm, asked_sm, place_vm, place_sm,
    owner_v, block_v, offset_v, frac_v, count_s, stack,
    load_sem, send_sem, recv_sem,
):
    az, rad, ax = lax.axis_index("az"), lax.axis_index("rad"), lax.axis_index("ax")
    n_az, n_rad, n_ax = lax.axis_size("az"), lax.axis_size("rad"), lax.axis_size("ax")
    up = (lax.rem(az + 1, n_az), rad, ax)
    down = (lax.rem(az + n_az - 1, n_az), rad, ax)
    partner = (az, 1 - rad, ax)
    fore = (az, rad, lax.rem(ax + 1, n_ax))
    aft = (az, rad, lax.rem(ax + n_ax - 1, n_ax))

    barrier = pltpu.get_barrier_semaphore()
    for target in (up, down, partner, fore, aft):
        pl.semaphore_signal(barrier, inc=1, device_id=target, device_id_type=MESH)

    loads = []

    def load(src, dst):
        copy = pltpu.make_async_copy(src, dst, load_sem.at[len(loads)])
        copy.start()
        loads.append(copy)
        return copy

    small = [load(owner, owner_v), load(block, block_v), load(offset, offset_v), load(frac, frac_v), load(count, count_s)]
    bulk = [load(vel, raw.at[0:3, 1 : CA + 1]), load(strain, raw.at[3:9, 1 : CA + 1])]
    tables = [load(lm_avg, own.at[0]), load(mm_avg, own.at[1])]
    later = [load(lm_avg, table.at[0, 0:LINES]), load(mm_avg, table.at[1, 0:LINES])]

    sent = []

    def send(src, dst, target):
        copy = pltpu.make_async_remote_copy(
            src_ref=src, dst_ref=dst, send_sem=send_sem.at[len(sent)], recv_sem=recv_sem.at[len(sent)],
            device_id=target, device_id_type=MESH,
        )
        copy.start()
        sent.append(copy)
        return copy

    for copy in small:
        copy.wait()
    own_id = owner_v[:, 0, :]
    wanted = block_v[:, 0, :]
    self_id = (az * n_rad + rad) * n_ax + ax
    down_id = (down[0] * n_rad + rad) * n_ax + ax
    up_id = (up[0] * n_rad + rad) * n_ax + ax
    rad_id = (az * n_rad + 1 - rad) * n_ax + ax
    line_no = lax.broadcasted_iota(jnp.int32, (CA, CR), 0) * CR + lax.broadcasted_iota(jnp.int32, (CA, CR), 1)
    live = line_no < count_s[self_id]
    hits = [live & (own_id == peer) for peer in (down_id, up_id, rad_id)]
    masks = jnp.concatenate([jnp.where(h, 1.0, 0.0) for h in hits], axis=0)
    row = lax.broadcasted_iota(jnp.int32, (CR, CR), 0)
    col = lax.broadcasted_iota(jnp.int32, (CR, CR), 1)
    prefix = jnp.dot(masks, jnp.where(row <= col, 1.0, 0.0), preferred_element_type=f32)
    totals = jnp.dot(masks, jnp.ones((CR, CR), f32), preferred_element_type=f32)
    row3 = lax.broadcasted_iota(jnp.int32, (3 * CA, 3 * CA), 0)
    col3 = lax.broadcasted_iota(jnp.int32, (3 * CA, 3 * CA), 1)
    before = jnp.where((row3 > col3) & (row3 // CA == col3 // CA), 1.0, 0.0)
    rank = (prefix + jnp.dot(before, totals, preferred_element_type=f32)).astype(jnp.int32) - 1
    slot = jnp.full((CA, CR), -1, jnp.int32)
    place = jnp.where(live, wanted, line_no)
    for k in range(3):
        here = rank[k * CA : (k + 1) * CA] + k * CAP
        slot = jnp.where(hits[k], here, slot)
        place = jnp.where(hits[k], here + LINES, place)
    place_vm[:, 0:CR] = place
    stack[...] = jnp.zeros((CX, CX), f32)
    stack[0:CA, 0:CR] = slot.astype(f32)
    stack[CA : 2 * CA, 0:CR] = wanted.astype(f32)
    stack[2 * CA : 3 * CA, 0:CR] = offset_v[:, 0, :].astype(f32)
    stack[3 * CA : 4 * CA, 0:CR] = frac_v[:, 0, :]
    turned = jnp.transpose(stack[...])[0:CR]
    columns_out[...] = turned
    slots = lax.broadcasted_iota(jnp.int32, (CR, CX), 1).astype(f32)
    found = [jnp.zeros((CR, CX), f32)] * 3
    for a in range(CA):
        at = jnp.broadcast_to(turned[:, a : a + 1], (CR, CX)) - slots
        number = jnp.broadcast_to(turned[:, CA + a : CA + a + 1], (CR, CX))
        for k in range(3):
            found[k] = jnp.where(at == float(k * CAP), number, found[k])
    for k in range(3):
        ask[k] = jnp.broadcast_to(jnp.sum(found[k], axis=0, keepdims=True), (8, CX)).astype(jnp.int32)
    to_place = pltpu.make_async_copy(place_vm, place_sm, load_sem.at[len(loads)])
    to_place.start()

    pl.semaphore_wait(barrier, 5)

    queries = [send(ask.at[0], asked_vm.at[0], down), send(ask.at[1], asked_vm.at[1], up), send(ask.at[2], asked_vm.at[2], partner)]
    halos = [
        send(strain.at[:, CA - 1], raw.at[3:9, 0], up),
        send(strain.at[:, 0], raw.at[3:9, CA + 1], down),
        send(vel.at[:, CA - 1], raw.at[0:3, 0], up),
        send(vel.at[:, 0], raw.at[0:3, CA + 1], down),
    ]

    lane = lax.broadcasted_iota(jnp.int32, (8, CX), 1)
    for copy in bulk:
        copy.wait()

    @pl.loop(0, CA)
    def pack(a):
        first = last = jnp.zeros((8, CX), f32)
        for g in range(GROUPS):
            for c in range(9):
                at = 9 * g + c
                moved = raw[c, a + 1, 8 * g : 8 * g + 8]
                moved = pltpu.roll(moved, at, 1) if at else moved
                first = jnp.where(lane == at, moved, first)
                last = jnp.where(lane == (at - 1) % CX, moved, last)
        col_send[0, a] = first
        col_send[1, a] = last

    sides = [send(col_send.at[0], cols.at[1, 1 : CA + 1], aft), send(col_send.at[1], cols.at[0, 1 : CA + 1], fore)]

    for copy in queries:
        copy.wait()
    to_asked = pltpu.make_async_copy(asked_vm, asked_sm, load_sem.at[len(loads) + 1])
    to_asked.start()
    for copy in tables:
        copy.wait()
    to_asked.wait()
    for copy in sides:
        copy.wait()
    corners = [
        send(cols.at[:, CA], cols.at[:, 0], up),
        send(cols.at[:, 1], cols.at[:, CA + 1], down),
    ]

    @pl.loop(0, 3 * (CAP // 8))
    def answer(step):
        k = step // (CAP // 8)
        base = (step % (CAP // 8)) * 8
        for j in range(8):
            number = jnp.clip(asked_sm[k, 0, base + j], 0, LINES - 1)
            for ch in range(2):
                reply[k, ch, pl.ds(base + j, 1)] = own[ch, pl.ds(number, 1)]

    replies = [
        send(reply.at[0], table.at[:, LINES : LINES + CAP], up),
        send(reply.at[1], table.at[:, LINES + CAP : LINES + 2 * CAP], down),
        send(reply.at[2], table.at[:, LINES + 2 * CAP : LINES + 3 * CAP], partner),
    ]

    keep_aft = jnp.where(ax > 0, 1.0, 0.0)
    keep_fore = jnp.where(ax < n_ax - 1, 1.0, 0.0)
    aft_lane = lax.rem(lane, 9) == 0

    def axial(l, ours):
        low, high = cols[0, l] * keep_aft, cols[1, l] * keep_fore
        ends = []
        for c in range(9):
            low_c = pltpu.roll(low, (1 - c) % CX, 1) if c != 1 else low
            high_c = pltpu.roll(high, CX - 1 - c, 1)
            ends.append(jnp.where(aft_lane, low_c, high_c))
        ends, _ = products(ends)
        for ch in range(NCH):
            halo_prod[ch] = ends[ch]
        for g in range(GROUPS):
            rows = slice(8 * g, 8 * g + 8)
            fields, norm = products([raw[c, l, rows] for c in range(9)])
            if ours:
                mag[l - 1, rows] = norm
            for ch in range(NCH):
                value = fields[ch]
                end = halo_prod[ch]
                end = pltpu.roll(end, CX - 9 * g, 1) if g else end
                left = jnp.where(lane == 0, end, pltpu.roll(value, 1, 1))
                right = jnp.where(lane == CX - 1, end, pltpu.roll(value, CX - 1, 1))
                ax_done[ch, l, rows] = (value + value) + (left + right)

    def azimuthal(ch, layers):
        edges = {}
        for g in range(GROUPS):
            rows = slice(8 * g, 8 * g + 8)
            value = {}
            for l in layers:
                for n in (l - 1, l, l + 1):
                    if n not in value:
                        value[n] = ax_done[ch, n, rows]
                out = (value[l] + value[l]) + (value[l - 1] + value[l + 1])
                az_done[ch, l - 1, rows] = out
                if g == 0:
                    edges[l] = out[0:1]
                if g == GROUPS - 1:
                    row_send[l - 1, pl.ds(ch, 1)] = jnp.where(rad == 0, out[7:8], edges[l])

    sub = lax.broadcasted_iota(jnp.int32, (CR, CX), 0)

    def radial(a):
        for ch in range(NCH):
            value = az_done[ch, a]
            halo = row_recv[a, ch : ch + 1]
            above = jnp.where(rad == 1, halo, 0.0)
            below = jnp.where(rad == 0, halo, 0.0)
            prior = jnp.where(sub == 0, above, pltpu.roll(value, 1, 0))
            after = jnp.where(sub == CR - 1, below, pltpu.roll(value, CR - 1, 0))
            rad_done[ch] = ((value + value) + (prior + after)) * (1.0 / 64.0)
        for g in range(GROUPS):
            rows = slice(8 * g, 8 * g + 8)
            lm, mm = contract([rad_done[ch, rows] for ch in range(NCH)])
            lm_here[a, rows] = lm
            mm_here[a, rows] = mm

    pl.loop(1, CA + 1)(lambda l: axial(l, True))
    inner = tuple(range(2, CA))
    pl.loop(0, NCH)(lambda ch: azimuthal(ch, inner))
    rows_in = [send(row_send.at[1 : CA - 1], row_recv.at[1 : CA - 1], partner)]
    rows_in[0].wait()
    pl.loop(1, CA - 1)(radial)

    for copy in halos + corners:
        copy.wait()
    pl.loop(0, 2)(lambda i: axial(i * (CA + 1), False))

    pl.loop(0, NCH)(lambda ch: azimuthal(ch, (1, CA)))
    rows_out = [send(row_send.at[0], row_recv.at[0], partner), send(row_send.at[CA - 1], row_recv.at[CA - 1], partner)]
    for copy in rows_out:
        copy.wait()

    @pl.loop(0, 2)
    def edge_radial(i):
        radial(i * (CA - 1))

    for copy in later + replies:
        copy.wait()
    to_place.wait()

    @pl.loop(0, LINES // 8)
    def put(step):
        a = step // GROUPS
        base = (step % GROUPS) * 8
        for j in range(8):
            number = jnp.clip(place_sm[a, base + j], 0, LINES + 3 * CAP - 1)
            for ch in range(2):
                lines[ch, pl.ds(step * 8 + j, 1)] = table[ch, pl.ds(number, 1)]


def relax_kernel(lines, lm_here, mm_here, mag, columns, lm_new, mm_new, eddy):
    cell = lax.broadcasted_iota(jnp.int32, (CR, CX), 1)
    for a in range(CA):
        shift = jnp.broadcast_to(columns[:, 2 * CA + a : 2 * CA + a + 1], (CR, CX)).astype(jnp.int32)
        weight = jnp.broadcast_to(columns[:, 3 * CA + a : 3 * CA + a + 1], (CR, CX))
        anchor = cell - shift
        left = jnp.maximum(anchor, 0)
        right = jnp.clip(anchor + 1, 0, CX - 1)
        upstream = []
        for ch in range(2):
            line = lines[ch, a * CR : (a + 1) * CR]
            upstream.append(
                (1.0 - weight) * jnp.take_along_axis(line, left, axis=1)
                + weight * jnp.take_along_axis(line, right, axis=1)
            )
        up_lm, up_mm = upstream
        theta = 0.5 * jnp.sqrt(jnp.sqrt(jnp.sqrt(jnp.maximum(up_lm, 0.0) * up_mm)))
        eps = theta / (1.0 + theta)
        lm = jnp.maximum(eps * lm_here[a] + (1.0 - eps) * up_lm, 0.0)
        mm = eps * mm_here[a] + (1.0 - eps) * up_mm
        lm_new[a] = lm
        mm_new[a] = mm
        eddy[a] = 0.25 * lm / mm * mag[a]


def on_device(velocity, strain_rate, lm_average, mm_average, source_owner, source_block, offset_cells, fraction, query_count):
    grid = (CA, CR, CX)
    line_form = (LINES, CX)
    flat = (CA, 1, CR)
    SDS = jax.ShapeDtypeStruct
    VMEM = pltpu.VMEM
    whole = pl.BlockSpec(memory_space=pltpu.VMEM)
    lines, lm_here, mm_here, mag, columns = pl.pallas_call(
        exchange_kernel,
        out_shape=[VMEM((2,) + line_form, f32), VMEM(grid, f32), VMEM(grid, f32), VMEM(grid, f32), VMEM((CR, CX), f32)],
        in_specs=[pl.BlockSpec(memory_space=pltpu.HBM)] * 9,
        out_specs=[whole] * 5,
        scratch_shapes=[
            VMEM((9, CA + 2, CR, CX), f32),
            VMEM((2, CA + 2, 8, CX), f32),
            VMEM((2, CA, 8, CX), f32),
            VMEM((NCH, 8, CX), f32),
            VMEM((NCH, CA + 2, CR, CX), f32),
            VMEM((NCH, CA, CR, CX), f32),
            VMEM((CA, 24, CX), f32),
            VMEM((CA, 24, CX), f32),
            VMEM((NCH, CR, CX), f32),
            VMEM((2,) + line_form, f32),
            VMEM((2, LINES + 3 * CAP, CX), f32),
            VMEM((3, 2, CAP, CX), f32),
            VMEM((3, 8, CX), jnp.int32),
            VMEM((3, 8, CX), jnp.int32),
            pltpu.SMEM((3, 8, CX), jnp.int32),
            VMEM((CA, CX), jnp.int32),
            pltpu.SMEM((CA, CX), jnp.int32),
            VMEM(flat, jnp.int32),
            VMEM(flat, jnp.int32),
            VMEM(flat, jnp.int32),
            VMEM(flat, f32),
            pltpu.SMEM(query_count.shape, jnp.int32),
            VMEM((CX, CX), f32),
            pltpu.SemaphoreType.DMA((16,)),
            pltpu.SemaphoreType.DMA((20,)),
            pltpu.SemaphoreType.DMA((20,)),
        ],
        compiler_params=pltpu.CompilerParams(collective_id=0, has_side_effects=True, vmem_limit_bytes=VMEM_LIMIT),
        name="exchange",
    )(*(pltpu.with_memory_space_constraint(x, pltpu.HBM) for x in (
        velocity, strain_rate, lm_average.reshape(line_form), mm_average.reshape(line_form),
        source_owner.reshape(flat), source_block.reshape(flat), offset_cells.reshape(flat), fraction.reshape(flat),
        query_count,
    )))
    return pl.pallas_call(
        relax_kernel,
        out_shape=[SDS(grid, f32)] * 3,
        in_specs=[whole] * 5,
        out_specs=[whole] * 3,
        compiler_params=pltpu.CompilerParams(vmem_limit_bytes=32 * 2**20),
        name="relax",
    )(lines, lm_here, mm_here, mag, columns)


def solution(mesh):
    cells, lines = P(None, "az", "rad", "ax"), P("az", "rad", "ax")
    return jax.shard_map(
        on_device,
        mesh=mesh,
        in_specs=(cells, cells) + (lines,) * 6 + (P(),),
        out_specs=(lines, lines, lines),
        check_vma=False,
    )
```

```python
import jax
import jax.numpy as jnp
from jax import lax
from jax.experimental import pallas as pl
from jax.experimental.pallas import tpu as pltpu
from jax.sharding import PartitionSpec as P

MESH = pl.DeviceIdType.MESH
pair_list = ((0, 0), (1, 1), (2, 2), (0, 1), (0, 2), (1, 2))
CA, CR, CX = 8, 64, 128
NCH = 21
LINES = CA * CR
CAP = LINES // 4
GROUPS = CR // 8
f32 = jnp.float32
VMEM_LIMIT = 48000 * 2**10


def strain_norm(s):
    normal = s[0] * s[0] + s[1] * s[1] + s[2] * s[2]
    shearing = s[3] * s[3] + s[4] * s[4] + s[5] * s[5]
    return jnp.sqrt(2.0 * normal + 4.0 * shearing)


def products(raw):
    vel, strain = raw[:3], raw[3:]
    magnitude = strain_norm(strain)
    fields = list(vel)
    fields += [vel[i] * vel[j] for i, j in pair_list]
    fields += strain
    fields += [magnitude * s for s in strain]
    return fields, magnitude


def contract(filtered):
    strain = [filtered[9 + c] for c in range(6)]
    four_norm = 4.0 * strain_norm(strain)
    sums = []
    for channels in ((0, 1, 2), (3, 4, 5)):
        lm = mm = None
        for c in channels:
            i, j = pair_list[c]
            leonard = filtered[3 + c] - filtered[i] * filtered[j]
            model = filtered[15 + c] - four_norm * strain[c]
            lm = leonard * model if lm is None else lm + leonard * model
            mm = model * model if mm is None else mm + model * model
        sums.append((lm, mm))
    (lm_a, mm_a), (lm_b, mm_b) = sums
    return 0.5 * lm_a + lm_b, 0.25 * mm_a + 0.5 * mm_b


def exchange_kernel(
    vel, strain, lm_avg, mm_avg, owner, block, offset, frac, count,
    lines, lm_here, mm_here, mag, columns_out,
    raw, cols, col_send, halo_prod, ax_done, az_done, row_send, row_recv, rad_done,
    own, table, reply, ask, asked_vm, asked_sm, place_vm, place_sm,
    owner_v, block_v, offset_v, frac_v, count_s, stack,
    load_sem, send_sem, recv_sem,
):
    az, rad, ax = lax.axis_index("az"), lax.axis_index("rad"), lax.axis_index("ax")
    n_az, n_rad, n_ax = lax.axis_size("az"), lax.axis_size("rad"), lax.axis_size("ax")
    up = (lax.rem(az + 1, n_az), rad, ax)
    down = (lax.rem(az + n_az - 1, n_az), rad, ax)
    partner = (az, 1 - rad, ax)
    fore = (az, rad, lax.rem(ax + 1, n_ax))
    aft = (az, rad, lax.rem(ax + n_ax - 1, n_ax))

    barrier = pltpu.get_barrier_semaphore()
    for target in (up, down, partner, fore, aft):
        pl.semaphore_signal(barrier, inc=1, device_id=target, device_id_type=MESH)

    loads = []

    def load(src, dst):
        copy = pltpu.make_async_copy(src, dst, load_sem.at[len(loads)])
        copy.start()
        loads.append(copy)
        return copy

    small = [load(owner, owner_v), load(block, block_v), load(offset, offset_v), load(frac, frac_v), load(count, count_s)]
    bulk = [load(vel, raw.at[0:3, 1 : CA + 1]), load(strain, raw.at[3:9, 1 : CA + 1])]
    tables = [load(lm_avg, own.at[0]), load(mm_avg, own.at[1])]
    later = [load(lm_avg, table.at[0, 0:LINES]), load(mm_avg, table.at[1, 0:LINES])]

    sent = []

    def send(src, dst, target):
        copy = pltpu.make_async_remote_copy(
            src_ref=src, dst_ref=dst, send_sem=send_sem.at[len(sent)], recv_sem=recv_sem.at[len(sent)],
            device_id=target, device_id_type=MESH,
        )
        copy.start()
        sent.append(copy)
        return copy

    lane = lax.broadcasted_iota(jnp.int32, (8, CX), 1)
    for copy in small:
        copy.wait()
    own_id = owner_v[:, 0, :]
    wanted = block_v[:, 0, :]
    self_id = (az * n_rad + rad) * n_ax + ax
    down_id = (down[0] * n_rad + rad) * n_ax + ax
    up_id = (up[0] * n_rad + rad) * n_ax + ax
    rad_id = (az * n_rad + 1 - rad) * n_ax + ax
    line_no = lax.broadcasted_iota(jnp.int32, (CA, CR), 0) * CR + lax.broadcasted_iota(jnp.int32, (CA, CR), 1)
    live = line_no < count_s[self_id]
    hits = [live & (own_id == peer) for peer in (down_id, up_id, rad_id)]
    masks = jnp.concatenate([jnp.where(h, 1.0, 0.0) for h in hits], axis=0)
    row = lax.broadcasted_iota(jnp.int32, (CR, CR), 0)
    col = lax.broadcasted_iota(jnp.int32, (CR, CR), 1)
    prefix = jnp.dot(masks, jnp.where(row <= col, 1.0, 0.0), preferred_element_type=f32)
    totals = jnp.dot(masks, jnp.ones((CR, CR), f32), preferred_element_type=f32)
    row3 = lax.broadcasted_iota(jnp.int32, (3 * CA, 3 * CA), 0)
    col3 = lax.broadcasted_iota(jnp.int32, (3 * CA, 3 * CA), 1)
    before = jnp.where((row3 > col3) & (row3 // CA == col3 // CA), 1.0, 0.0)
    rank = (prefix + jnp.dot(before, totals, preferred_element_type=f32)).astype(jnp.int32) - 1
    slot = jnp.full((CA, CR), -1, jnp.int32)
    place = jnp.where(live, wanted, line_no)
    for k in range(3):
        here = rank[k * CA : (k + 1) * CA] + k * CAP
        slot = jnp.where(hits[k], here, slot)
        place = jnp.where(hits[k], here + LINES, place)
    place_vm[:, 0:CR] = place
    stack[...] = jnp.zeros((CX, CX), f32)
    stack[0:CA, 0:CR] = slot.astype(f32)
    stack[CA : 2 * CA, 0:CR] = wanted.astype(f32)
    stack[2 * CA : 3 * CA, 0:CR] = offset_v[:, 0, :].astype(f32)
    stack[3 * CA : 4 * CA, 0:CR] = frac_v[:, 0, :]
    turned = jnp.transpose(stack[...])[0:CR]
    columns_out[...] = turned
    slots = lax.broadcasted_iota(jnp.int32, (CR, CX), 1).astype(f32)
    found = [jnp.zeros((CR, CX), f32)] * 3
    for a in range(CA):
        at = jnp.broadcast_to(turned[:, a : a + 1], (CR, CX)) - slots
        number = jnp.broadcast_to(turned[:, CA + a : CA + a + 1], (CR, CX))
        for k in range(3):
            found[k] = jnp.where(at == float(k * CAP), number, found[k])
    for k in range(3):
        ask[k] = jnp.broadcast_to(jnp.sum(found[k], axis=0, keepdims=True), (8, CX)).astype(jnp.int32)
    to_place = pltpu.make_async_copy(place_vm, place_sm, load_sem.at[len(loads)])
    to_place.start()


    for copy in bulk:
        copy.wait()

    @pl.loop(0, CA)
    def pack(a):
        first = last = jnp.zeros((8, CX), f32)
        for g in range(GROUPS):
            for c in range(9):
                at = 9 * g + c
                moved = raw[c, a + 1, 8 * g : 8 * g + 8]
                moved = pltpu.roll(moved, at, 1) if at else moved
                first = jnp.where(lane == at, moved, first)
                last = jnp.where(lane == (at - 1) % CX, moved, last)
        col_send[0, a] = first
        col_send[1, a] = last

    pl.semaphore_wait(barrier, 5)

    queries = [
        send(ask.at[0], asked_vm.at[0], down),
        send(ask.at[1], asked_vm.at[1], up),
        send(ask.at[2], asked_vm.at[2], partner),
    ]
    sides = [
        send(col_send.at[0], cols.at[1, 1 : CA + 1], aft),
        send(col_send.at[1], cols.at[0, 1 : CA + 1], fore),
    ]
    halos = [
        send(vel.at[:, CA - 1], raw.at[0:3, 0], up),
        send(vel.at[:, 0], raw.at[0:3, CA + 1], down),
    ]
    halos += [
        send(strain.at[:, CA - 1], raw.at[3:9, 0], up),
        send(strain.at[:, 0], raw.at[3:9, CA + 1], down),
    ]

    for copy in queries:
        copy.wait()
    to_asked = pltpu.make_async_copy(asked_vm, asked_sm, load_sem.at[len(loads) + 1])
    to_asked.start()
    for copy in tables:
        copy.wait()
    to_asked.wait()

    @pl.loop(0, 3 * (CAP // 64))
    def answer(step):
        k = step // (CAP // 64)
        base = (step % (CAP // 64)) * 64
        for j in range(64):
            number = jnp.clip(asked_sm[k, 0, base + j], 0, LINES - 1)
            for ch in range(2):
                reply[k, ch, pl.ds(base + j, 1)] = own[ch, pl.ds(number, 1)]

    for copy in sides:
        copy.wait()
    corners = [
        send(cols.at[:, CA], cols.at[:, 0], up),
        send(cols.at[:, 1], cols.at[:, CA + 1], down),
    ]
    replies = [
        send(reply.at[0], table.at[:, LINES : LINES + CAP], up),
        send(reply.at[1], table.at[:, LINES + CAP : LINES + 2 * CAP], down),
        send(reply.at[2], table.at[:, LINES + 2 * CAP : LINES + 3 * CAP], partner),
    ]

    keep_aft = jnp.where(ax > 0, 1.0, 0.0)
    keep_fore = jnp.where(ax < n_ax - 1, 1.0, 0.0)
    aft_lane = lax.rem(lane, 9) == 0

    def axial(l, ours):
        low, high = cols[0, l] * keep_aft, cols[1, l] * keep_fore
        ends = []
        for c in range(9):
            low_c = pltpu.roll(low, (1 - c) % CX, 1) if c != 1 else low
            high_c = pltpu.roll(high, CX - 1 - c, 1)
            ends.append(jnp.where(aft_lane, low_c, high_c))
        ends, _ = products(ends)
        for ch in range(NCH):
            halo_prod[ch] = ends[ch]
        for g in range(GROUPS):
            rows = slice(8 * g, 8 * g + 8)
            fields, norm = products([raw[c, l, rows] for c in range(9)])
            if ours:
                mag[l - 1, rows] = norm
            for ch in range(NCH):
                value = fields[ch]
                end = halo_prod[ch]
                end = pltpu.roll(end, CX - 9 * g, 1) if g else end
                left = jnp.where(lane == 0, end, pltpu.roll(value, 1, 1))
                right = jnp.where(lane == CX - 1, end, pltpu.roll(value, CX - 1, 1))
                ax_done[ch, l, rows] = (value + value) + (left + right)

    def azimuthal(ch, layers):
        edges = {}
        for g in range(GROUPS):
            rows = slice(8 * g, 8 * g + 8)
            value = {}
            for l in layers:
                for n in (l - 1, l, l + 1):
                    if n not in value:
                        value[n] = ax_done[ch, n, rows]
                out = (value[l] + value[l]) + (value[l - 1] + value[l + 1])
                az_done[ch, l - 1, rows] = out
                if g == 0:
                    edges[l] = out[0:1]
                if g == GROUPS - 1:
                    row_send[l - 1, pl.ds(ch, 1)] = jnp.where(rad == 0, out[7:8], edges[l])

    sub = lax.broadcasted_iota(jnp.int32, (CR, CX), 0)

    def radial(a):
        for ch in range(NCH):
            value = az_done[ch, a]
            halo = row_recv[a, ch : ch + 1]
            above = jnp.where(rad == 1, halo, 0.0)
            below = jnp.where(rad == 0, halo, 0.0)
            prior = jnp.where(sub == 0, above, pltpu.roll(value, 1, 0))
            after = jnp.where(sub == CR - 1, below, pltpu.roll(value, CR - 1, 0))
            rad_done[ch] = ((value + value) + (prior + after)) * (1.0 / 64.0)
        for g in range(GROUPS):
            rows = slice(8 * g, 8 * g + 8)
            lm, mm = contract([rad_done[ch, rows] for ch in range(NCH)])
            lm_here[a, rows] = lm
            mm_here[a, rows] = mm

    pl.loop(1, CA + 1)(lambda l: axial(l, True))
    inner = tuple(range(2, CA))
    pl.loop(0, NCH)(lambda ch: azimuthal(ch, inner))
    rows_in = [send(row_send.at[1 : CA - 1], row_recv.at[1 : CA - 1], partner)]
    rows_in[0].wait()
    pl.loop(1, CA - 1)(radial)

    for copy in halos + corners:
        copy.wait()
    pl.loop(0, 2)(lambda i: axial(i * (CA + 1), False))

    pl.loop(0, NCH)(lambda ch: azimuthal(ch, (1, CA)))
    rows_out = [send(row_send.at[0], row_recv.at[0], partner), send(row_send.at[CA - 1], row_recv.at[CA - 1], partner)]
    for copy in later + replies:
        copy.wait()
    to_place.wait()

    @pl.loop(0, LINES // 64)
    def put(step):
        a = step // (CR // 64)
        base = (step % (CR // 64)) * 64
        for j in range(64):
            number = jnp.clip(place_sm[a, base + j], 0, LINES + 3 * CAP - 1)
            for ch in range(2):
                lines[ch, pl.ds(step * 64 + j, 1)] = table[ch, pl.ds(number, 1)]


    for copy in rows_out:
        copy.wait()

    @pl.loop(0, 2)
    def edge_radial(i):
        radial(i * (CA - 1))

def relax_kernel(lines, lm_here, mm_here, mag, columns, lm_new, mm_new, eddy):
    cell = lax.broadcasted_iota(jnp.int32, (CR, CX), 1)
    for a in range(CA):
        shift = jnp.broadcast_to(columns[:, 2 * CA + a : 2 * CA + a + 1], (CR, CX)).astype(jnp.int32)
        weight = jnp.broadcast_to(columns[:, 3 * CA + a : 3 * CA + a + 1], (CR, CX))
        anchor = cell - shift
        left = jnp.maximum(anchor, 0)
        right = jnp.clip(anchor + 1, 0, CX - 1)
        upstream = []
        for ch in range(2):
            line = lines[ch, a * CR : (a + 1) * CR]
            upstream.append(
                (1.0 - weight) * jnp.take_along_axis(line, left, axis=1)
                + weight * jnp.take_along_axis(line, right, axis=1)
            )
        up_lm, up_mm = upstream
        theta = 0.5 * jnp.sqrt(jnp.sqrt(jnp.sqrt(jnp.maximum(up_lm, 0.0) * up_mm)))
        eps = theta / (1.0 + theta)
        lm = jnp.maximum(eps * lm_here[a] + (1.0 - eps) * up_lm, 0.0)
        mm = eps * mm_here[a] + (1.0 - eps) * up_mm
        lm_new[a] = lm
        mm_new[a] = mm
        eddy[a] = 0.25 * lm / mm * mag[a]


def on_device(velocity, strain_rate, lm_average, mm_average, source_owner, source_block, offset_cells, fraction, query_count):
    grid = (CA, CR, CX)
    line_form = (LINES, CX)
    flat = (CA, 1, CR)
    SDS = jax.ShapeDtypeStruct
    VMEM = pltpu.VMEM
    whole = pl.BlockSpec(memory_space=pltpu.VMEM)
    lines, lm_here, mm_here, mag, columns = pl.pallas_call(
        exchange_kernel,
        out_shape=[VMEM((2,) + line_form, f32), VMEM(grid, f32), VMEM(grid, f32), VMEM(grid, f32), VMEM((CR, CX), f32)],
        in_specs=[pl.BlockSpec(memory_space=pltpu.HBM)] * 9,
        out_specs=[whole] * 5,
        scratch_shapes=[
            VMEM((9, CA + 2, CR, CX), f32),
            VMEM((2, CA + 2, 8, CX), f32),
            VMEM((2, CA, 8, CX), f32),
            VMEM((NCH, 8, CX), f32),
            VMEM((NCH, CA + 2, CR, CX), f32),
            VMEM((NCH, CA, CR, CX), f32),
            VMEM((CA, 24, CX), f32),
            VMEM((CA, 24, CX), f32),
            VMEM((NCH, CR, CX), f32),
            VMEM((2,) + line_form, f32),
            VMEM((2, LINES + 3 * CAP, CX), f32),
            VMEM((3, 2, CAP, CX), f32),
            VMEM((3, 8, CX), jnp.int32),
            VMEM((3, 8, CX), jnp.int32),
            pltpu.SMEM((3, 8, CX), jnp.int32),
            VMEM((CA, CX), jnp.int32),
            pltpu.SMEM((CA, CX), jnp.int32),
            VMEM(flat, jnp.int32),
            VMEM(flat, jnp.int32),
            VMEM(flat, jnp.int32),
            VMEM(flat, f32),
            pltpu.SMEM(query_count.shape, jnp.int32),
            VMEM((CX, CX), f32),
            pltpu.SemaphoreType.DMA((16,)),
            pltpu.SemaphoreType.DMA((20,)),
            pltpu.SemaphoreType.DMA((20,)),
        ],
        compiler_params=pltpu.CompilerParams(collective_id=0, has_side_effects=True, vmem_limit_bytes=VMEM_LIMIT),
        name="exchange",
    )(*(pltpu.with_memory_space_constraint(x, pltpu.HBM) for x in (
        velocity, strain_rate, lm_average.reshape(line_form), mm_average.reshape(line_form),
        source_owner.reshape(flat), source_block.reshape(flat), offset_cells.reshape(flat), fraction.reshape(flat),
        query_count,
    )))
    return pl.pallas_call(
        relax_kernel,
        out_shape=[SDS(grid, f32)] * 3,
        in_specs=[whole] * 5,
        out_specs=[whole] * 3,
        compiler_params=pltpu.CompilerParams(vmem_limit_bytes=32 * 2**20),
        name="relax",
    )(lines, lm_here, mm_here, mag, columns)


def solution(mesh):
    cells, lines = P(None, "az", "rad", "ax"), P("az", "rad", "ax")
    return jax.shard_map(
        on_device,
        mesh=mesh,
        in_specs=(cells, cells) + (lines,) * 6 + (P(),),
        out_specs=(lines, lines, lines),
        check_vma=False,
    )
```

```python
import jax
import jax.numpy as jnp
from jax import lax
from jax.experimental import pallas as pl
from jax.experimental.pallas import tpu as pltpu
from jax.sharding import PartitionSpec as P

MESH = pl.DeviceIdType.MESH
pair_list = ((0, 0), (1, 1), (2, 2), (0, 1), (0, 2), (1, 2))
CA, CR, CX = 8, 64, 128
NCH = 21
LINES = CA * CR
CAP = LINES // 4
GROUPS = CR // 8
f32 = jnp.float32
VMEM_LIMIT = 48000 * 2**10


def strain_norm(s):
    normal = s[0] * s[0] + s[1] * s[1] + s[2] * s[2]
    shearing = s[3] * s[3] + s[4] * s[4] + s[5] * s[5]
    return jnp.sqrt(2.0 * normal + 4.0 * shearing)


def products(raw):
    vel, strain = raw[:3], raw[3:]
    magnitude = strain_norm(strain)
    fields = list(vel)
    fields += [vel[i] * vel[j] for i, j in pair_list]
    fields += strain
    fields += [magnitude * s for s in strain]
    return fields, magnitude


def contract(filtered):
    strain = [filtered[9 + c] for c in range(6)]
    four_norm = 4.0 * strain_norm(strain)
    sums = []
    for channels in ((0, 1, 2), (3, 4, 5)):
        lm = mm = None
        for c in channels:
            i, j = pair_list[c]
            leonard = filtered[3 + c] - filtered[i] * filtered[j]
            model = filtered[15 + c] - four_norm * strain[c]
            lm = leonard * model if lm is None else lm + leonard * model
            mm = model * model if mm is None else mm + model * model
        sums.append((lm, mm))
    (lm_a, mm_a), (lm_b, mm_b) = sums
    return 0.5 * lm_a + lm_b, 0.25 * mm_a + 0.5 * mm_b


def exchange_kernel(
    vel, strain, lm_avg, mm_avg, owner, block, offset, frac, count,
    lines, lm_here, mm_here, mag, columns_out,
    raw, cols, col_send, ax_done, az_done, row_send, row_recv, rad_done,
    own, table, reply, ask, asked_vm, asked_sm, place_vm, place_sm,
    owner_v, block_v, offset_v, frac_v, count_s, stack,
    load_sem, send_sem, recv_sem,
):
    az, rad, ax = lax.axis_index("az"), lax.axis_index("rad"), lax.axis_index("ax")
    n_az, n_rad, n_ax = lax.axis_size("az"), lax.axis_size("rad"), lax.axis_size("ax")
    up = (lax.rem(az + 1, n_az), rad, ax)
    down = (lax.rem(az + n_az - 1, n_az), rad, ax)
    partner = (az, 1 - rad, ax)
    fore = (az, rad, lax.rem(ax + 1, n_ax))
    aft = (az, rad, lax.rem(ax + n_ax - 1, n_ax))

    barrier = pltpu.get_barrier_semaphore()
    for target in (up, down, partner, fore, aft):
        pl.semaphore_signal(barrier, inc=1, device_id=target, device_id_type=MESH)

    loads = []

    def load(src, dst):
        copy = pltpu.make_async_copy(src, dst, load_sem.at[len(loads)])
        copy.start()
        loads.append(copy)
        return copy

    small = [load(owner, owner_v), load(block, block_v), load(offset, offset_v), load(frac, frac_v), load(count, count_s)]
    bulk = [load(vel, raw.at[0:3, 1 : CA + 1]), load(strain, raw.at[3:9, 1 : CA + 1])]
    tables = [load(lm_avg, own.at[0]), load(mm_avg, own.at[1])]
    later = [load(lm_avg, table.at[0, 0:LINES]), load(mm_avg, table.at[1, 0:LINES])]

    sent = []

    def send(src, dst, target):
        copy = pltpu.make_async_remote_copy(
            src_ref=src, dst_ref=dst, send_sem=send_sem.at[len(sent)], recv_sem=recv_sem.at[len(sent)],
            device_id=target, device_id_type=MESH,
        )
        copy.start()
        sent.append(copy)
        return copy

    halos = []
    lane = lax.broadcasted_iota(jnp.int32, (8, CX), 1)
    for copy in small:
        copy.wait()
    own_id = owner_v[:, 0, :]
    wanted = block_v[:, 0, :]
    self_id = (az * n_rad + rad) * n_ax + ax
    down_id = (down[0] * n_rad + rad) * n_ax + ax
    up_id = (up[0] * n_rad + rad) * n_ax + ax
    rad_id = (az * n_rad + 1 - rad) * n_ax + ax
    line_no = lax.broadcasted_iota(jnp.int32, (CA, CR), 0) * CR + lax.broadcasted_iota(jnp.int32, (CA, CR), 1)
    live = line_no < count_s[self_id]
    hits = [live & (own_id == peer) for peer in (down_id, up_id, rad_id)]
    masks = jnp.concatenate([jnp.where(h, 1.0, 0.0) for h in hits], axis=0)
    row = lax.broadcasted_iota(jnp.int32, (CR, CR), 0)
    col = lax.broadcasted_iota(jnp.int32, (CR, CR), 1)
    prefix = jnp.dot(masks, jnp.where(row <= col, 1.0, 0.0), preferred_element_type=f32)
    totals = jnp.dot(masks, jnp.ones((CR, CR), f32), preferred_element_type=f32)
    row3 = lax.broadcasted_iota(jnp.int32, (3 * CA, 3 * CA), 0)
    col3 = lax.broadcasted_iota(jnp.int32, (3 * CA, 3 * CA), 1)
    before = jnp.where((row3 > col3) & (row3 // CA == col3 // CA), 1.0, 0.0)
    rank = (prefix + jnp.dot(before, totals, preferred_element_type=f32)).astype(jnp.int32) - 1
    slot = jnp.full((CA, CR), -1, jnp.int32)
    place = jnp.where(live, wanted, line_no)
    for k in range(3):
        here = rank[k * CA : (k + 1) * CA] + k * CAP
        slot = jnp.where(hits[k], here, slot)
        place = jnp.where(hits[k], here + LINES, place)
    place_vm[:, 0:CR] = place
    stack[...] = jnp.zeros((CX, CX), f32)
    stack[0:CA, 0:CR] = slot.astype(f32)
    stack[CA : 2 * CA, 0:CR] = wanted.astype(f32)
    stack[2 * CA : 3 * CA, 0:CR] = offset_v[:, 0, :].astype(f32)
    stack[3 * CA : 4 * CA, 0:CR] = frac_v[:, 0, :]
    turned = jnp.transpose(stack[...])[0:CR]
    columns_out[...] = turned
    slots = lax.broadcasted_iota(jnp.int32, (CR, CX), 1).astype(f32)
    found = [jnp.zeros((CR, CX), f32)] * 3
    for a in range(CA):
        at = jnp.broadcast_to(turned[:, a : a + 1], (CR, CX)) - slots
        number = jnp.broadcast_to(turned[:, CA + a : CA + a + 1], (CR, CX))
        for k in range(3):
            found[k] = jnp.where(at == float(k * CAP), number, found[k])
    for k in range(3):
        ask[k] = jnp.broadcast_to(jnp.sum(found[k], axis=0, keepdims=True), (8, CX)).astype(jnp.int32)
    to_place = pltpu.make_async_copy(place_vm, place_sm, load_sem.at[len(loads)])
    to_place.start()


    for copy in bulk:
        copy.wait()

    @pl.loop(0, CA)
    def pack(a):
        first = last = jnp.zeros((8, CX), f32)
        for g in range(GROUPS):
            for c in range(9):
                at = 9 * g + c
                moved = raw[c, a + 1, 8 * g : 8 * g + 8]
                moved = pltpu.roll(moved, at, 1) if at else moved
                first = jnp.where(lane == at, moved, first)
                last = jnp.where(lane == (at - 1) % CX, moved, last)
        col_send[0, a] = first
        col_send[1, a] = last

    pl.semaphore_wait(barrier, 5)

    queries = [
        send(ask.at[0], asked_vm.at[0], down),
        send(ask.at[1], asked_vm.at[1], up),
        send(ask.at[2], asked_vm.at[2], partner),
    ]
    sides = [
        send(col_send.at[0], cols.at[1, 1 : CA + 1], aft),
        send(col_send.at[1], cols.at[0, 1 : CA + 1], fore),
    ]
    halos += [
        send(vel.at[:, CA - 1], raw.at[0:3, 0], up),
        send(vel.at[:, 0], raw.at[0:3, CA + 1], down),
    ]
    halos += [
        send(strain.at[:, CA - 1], raw.at[3:9, 0], up),
        send(strain.at[:, 0], raw.at[3:9, CA + 1], down),
    ]

    for copy in queries:
        copy.wait()
    to_asked = pltpu.make_async_copy(asked_vm, asked_sm, load_sem.at[len(loads) + 1])
    to_asked.start()
    for copy in tables:
        copy.wait()
    to_asked.wait()

    @pl.loop(0, 3 * (CAP // 64))
    def answer(step):
        k = step // (CAP // 64)
        base = (step % (CAP // 64)) * 64
        for j in range(64):
            number = jnp.clip(asked_sm[k, 0, base + j], 0, LINES - 1)
            for ch in range(2):
                reply[k, ch, pl.ds(base + j, 1)] = own[ch, pl.ds(number, 1)]

    for copy in sides:
        copy.wait()
    corners = [
        send(cols.at[:, CA], cols.at[:, 0], up),
        send(cols.at[:, 1], cols.at[:, CA + 1], down),
    ]
    replies = [
        send(reply.at[0], table.at[:, LINES : LINES + CAP], up),
        send(reply.at[1], table.at[:, LINES + CAP : LINES + 2 * CAP], down),
        send(reply.at[2], table.at[:, LINES + 2 * CAP : LINES + 3 * CAP], partner),
    ]

    keep_aft = jnp.where(ax > 0, 1.0, 0.0)
    keep_fore = jnp.where(ax < n_ax - 1, 1.0, 0.0)
    aft_lane = lax.rem(lane, 9) == 0

    def axial(l, ours):
        low, high = cols[0, l] * keep_aft, cols[1, l] * keep_fore
        ends = []
        for c in range(9):
            low_c = pltpu.roll(low, (1 - c) % CX, 1) if c != 1 else low
            high_c = pltpu.roll(high, CX - 1 - c, 1)
            ends.append(jnp.where(aft_lane, low_c, high_c))
        for g in range(GROUPS):
            rows = slice(8 * g, 8 * g + 8)
            here, behind, ahead = [], [], []
            for c in range(9):
                value = raw[c, l, rows]
                end = pltpu.roll(ends[c], CX - 9 * g, 1) if g else ends[c]
                here.append(value)
                behind.append(jnp.where(lane == 0, end, pltpu.roll(value, 1, 1)))
                ahead.append(jnp.where(lane == CX - 1, end, pltpu.roll(value, CX - 1, 1)))
            here, norm = products(here)
            behind, ahead = products(behind)[0], products(ahead)[0]
            if ours:
                mag[l - 1, rows] = norm
            for ch in range(NCH):
                ax_done[ch, l, rows] = (here[ch] + here[ch]) + (behind[ch] + ahead[ch])

    def azimuthal(ch, layers):
        edges = {}
        for g in range(GROUPS):
            rows = slice(8 * g, 8 * g + 8)
            value = {}
            for l in layers:
                for n in (l - 1, l, l + 1):
                    if n not in value:
                        value[n] = ax_done[ch, n, rows]
                out = (value[l] + value[l]) + (value[l - 1] + value[l + 1])
                az_done[ch, l - 1, 8 * g + 8 : 8 * g + 16] = out
                if g == 0:
                    edges[l] = out[0:1]
                if g == GROUPS - 1:
                    row_send[l - 1, pl.ds(ch, 1)] = jnp.where(rad == 0, out[7:8], edges[l])

    def radial(a):
        for ch in range(NCH):
            value = az_done[ch, a, 8 : CR + 8]
            halo = row_recv[a, ch : ch + 1]
            above = jnp.where(rad == 1, halo, 0.0)
            below = jnp.where(rad == 0, halo, 0.0)
            az_done[ch, a, 7:8] = above
            az_done[ch, a, CR + 8 : CR + 9] = below
            prior = az_done[ch, a, 7 : CR + 7]
            after = az_done[ch, a, 9 : CR + 9]
            rad_done[ch] = ((value + value) + (prior + after)) * (1.0 / 64.0)
        for g in range(GROUPS):
            rows = slice(8 * g, 8 * g + 8)
            lm, mm = contract([rad_done[ch, rows] for ch in range(NCH)])
            lm_here[a, rows] = lm
            mm_here[a, rows] = mm

    pl.loop(1, CA + 1)(lambda l: axial(l, True))
    inner = tuple(range(2, CA))
    pl.loop(0, NCH)(lambda ch: azimuthal(ch, inner))
    rows_in = [send(row_send.at[1 : CA - 1], row_recv.at[1 : CA - 1], partner)]
    rows_in[0].wait()
    pl.loop(1, CA - 1)(radial)

    for copy in halos + corners:
        copy.wait()
    pl.loop(0, 2)(lambda i: axial(i * (CA + 1), False))

    pl.loop(0, NCH)(lambda ch: azimuthal(ch, (1, CA)))
    rows_out = [send(row_send.at[0], row_recv.at[0], partner), send(row_send.at[CA - 1], row_recv.at[CA - 1], partner)]
    for copy in later + replies:
        copy.wait()
    to_place.wait()

    @pl.loop(0, LINES // 64)
    def put(step):
        a = step // (CR // 64)
        base = (step % (CR // 64)) * 64
        for j in range(64):
            number = jnp.clip(place_sm[a, base + j], 0, LINES + 3 * CAP - 1)
            for ch in range(2):
                lines[ch, pl.ds(step * 64 + j, 1)] = table[ch, pl.ds(number, 1)]


    for copy in rows_out:
        copy.wait()

    @pl.loop(0, 2)
    def edge_radial(i):
        radial(i * (CA - 1))

def relax_kernel(lines, lm_here, mm_here, mag, columns, lm_new, mm_new, eddy):
    cell = lax.broadcasted_iota(jnp.int32, (CR, CX), 1)
    for a in range(CA):
        shift = jnp.broadcast_to(columns[:, 2 * CA + a : 2 * CA + a + 1], (CR, CX)).astype(jnp.int32)
        weight = jnp.broadcast_to(columns[:, 3 * CA + a : 3 * CA + a + 1], (CR, CX))
        anchor = cell - shift
        left = jnp.maximum(anchor, 0)
        right = jnp.clip(anchor + 1, 0, CX - 1)
        upstream = []
        for ch in range(2):
            line = lines[ch, a * CR : (a + 1) * CR]
            upstream.append(
                (1.0 - weight) * jnp.take_along_axis(line, left, axis=1)
                + weight * jnp.take_along_axis(line, right, axis=1)
            )
        up_lm, up_mm = upstream
        theta = 0.5 * jnp.sqrt(jnp.sqrt(jnp.sqrt(jnp.maximum(up_lm, 0.0) * up_mm)))
        eps = theta / (1.0 + theta)
        lm = jnp.maximum(eps * lm_here[a] + (1.0 - eps) * up_lm, 0.0)
        mm = eps * mm_here[a] + (1.0 - eps) * up_mm
        lm_new[a] = lm
        mm_new[a] = mm
        eddy[a] = 0.25 * lm / mm * mag[a]


def on_device(velocity, strain_rate, lm_average, mm_average, source_owner, source_block, offset_cells, fraction, query_count):
    grid = (CA, CR, CX)
    line_form = (LINES, CX)
    flat = (CA, 1, CR)
    SDS = jax.ShapeDtypeStruct
    VMEM = pltpu.VMEM
    whole = pl.BlockSpec(memory_space=pltpu.VMEM)
    lines, lm_here, mm_here, mag, columns = pl.pallas_call(
        exchange_kernel,
        out_shape=[VMEM((2,) + line_form, f32), VMEM(grid, f32), VMEM(grid, f32), VMEM(grid, f32), VMEM((CR, CX), f32)],
        in_specs=[pl.BlockSpec(memory_space=pltpu.HBM)] * 9,
        out_specs=[whole] * 5,
        scratch_shapes=[
            VMEM((9, CA + 2, CR, CX), f32),
            VMEM((2, CA + 2, 8, CX), f32),
            VMEM((2, CA, 8, CX), f32),
            VMEM((NCH, CA + 2, CR, CX), f32),
            VMEM((NCH, CA, CR + 16, CX), f32),
            VMEM((CA, 24, CX), f32),
            VMEM((CA, 24, CX), f32),
            VMEM((NCH, CR, CX), f32),
            VMEM((2,) + line_form, f32),
            VMEM((2, LINES + 3 * CAP, CX), f32),
            VMEM((3, 2, CAP, CX), f32),
            VMEM((3, 8, CX), jnp.int32),
            VMEM((3, 8, CX), jnp.int32),
            pltpu.SMEM((3, 8, CX), jnp.int32),
            VMEM((CA, CX), jnp.int32),
            pltpu.SMEM((CA, CX), jnp.int32),
            VMEM(flat, jnp.int32),
            VMEM(flat, jnp.int32),
            VMEM(flat, jnp.int32),
            VMEM(flat, f32),
            pltpu.SMEM(query_count.shape, jnp.int32),
            VMEM((CX, CX), f32),
            pltpu.SemaphoreType.DMA((16,)),
            pltpu.SemaphoreType.DMA((20,)),
            pltpu.SemaphoreType.DMA((20,)),
        ],
        compiler_params=pltpu.CompilerParams(collective_id=0, has_side_effects=True, vmem_limit_bytes=VMEM_LIMIT),
        name="exchange",
    )(*(pltpu.with_memory_space_constraint(x, pltpu.HBM) for x in (
        velocity, strain_rate, lm_average.reshape(line_form), mm_average.reshape(line_form),
        source_owner.reshape(flat), source_block.reshape(flat), offset_cells.reshape(flat), fraction.reshape(flat),
        query_count,
    )))
    return pl.pallas_call(
        relax_kernel,
        out_shape=[SDS(grid, f32)] * 3,
        in_specs=[whole] * 5,
        out_specs=[whole] * 3,
        compiler_params=pltpu.CompilerParams(vmem_limit_bytes=32 * 2**20),
        name="relax",
    )(lines, lm_here, mm_here, mag, columns)


def solution(mesh):
    cells, lines = P(None, "az", "rad", "ax"), P("az", "rad", "ax")
    return jax.shard_map(
        on_device,
        mesh=mesh,
        in_specs=(cells, cells) + (lines,) * 6 + (P(),),
        out_specs=(lines, lines, lines),
        check_vma=False,
    )
```

```python
import jax
import jax.numpy as jnp
from jax import lax
from jax.experimental import pallas as pl
from jax.experimental.pallas import tpu as pltpu
from jax.sharding import PartitionSpec as P

MESH = pl.DeviceIdType.MESH
pair_list = ((0, 0), (1, 1), (2, 2), (0, 1), (0, 2), (1, 2))
CA, CR, CX = 8, 64, 128
NCH = 21
LINES = CA * CR
CAP = LINES // 4
GROUPS = CR // 8
f32 = jnp.float32
VMEM_LIMIT = 48000 * 2**10


def strain_norm(s):
    normal = s[0] * s[0] + s[1] * s[1] + s[2] * s[2]
    shearing = s[3] * s[3] + s[4] * s[4] + s[5] * s[5]
    return jnp.sqrt(2.0 * normal + 4.0 * shearing)


def products(raw):
    vel, strain = raw[:3], raw[3:]
    magnitude = strain_norm(strain)
    fields = list(vel)
    fields += [vel[i] * vel[j] for i, j in pair_list]
    fields += strain
    fields += [magnitude * s for s in strain]
    return fields, magnitude


def contract(filtered):
    strain = [filtered[9 + c] for c in range(6)]
    four_norm = 4.0 * strain_norm(strain)
    sums = []
    for channels in ((0, 1, 2), (3, 4, 5)):
        lm = mm = None
        for c in channels:
            i, j = pair_list[c]
            leonard = filtered[3 + c] - filtered[i] * filtered[j]
            model = filtered[15 + c] - four_norm * strain[c]
            lm = leonard * model if lm is None else lm + leonard * model
            mm = model * model if mm is None else mm + model * model
        sums.append((lm, mm))
    (lm_a, mm_a), (lm_b, mm_b) = sums
    return 0.5 * lm_a + lm_b, 0.25 * mm_a + 0.5 * mm_b


def exchange_kernel(
    vel, strain, lm_avg, mm_avg, owner, block, offset, frac, count,
    upstream, lm_here, mm_here, mag,
    lines, columns,
    raw, cols, col_send, ax_done, az_done, row_send, row_recv, rad_done,
    own, table, reply, ask, asked_vm, asked_sm, place_vm, place_sm,
    owner_v, block_v, offset_v, frac_v, count_s, stack,
    load_sem, send_sem, recv_sem,
):
    az, rad, ax = lax.axis_index("az"), lax.axis_index("rad"), lax.axis_index("ax")
    n_az, n_rad, n_ax = lax.axis_size("az"), lax.axis_size("rad"), lax.axis_size("ax")
    up = (lax.rem(az + 1, n_az), rad, ax)
    down = (lax.rem(az + n_az - 1, n_az), rad, ax)
    partner = (az, 1 - rad, ax)
    fore = (az, rad, lax.rem(ax + 1, n_ax))
    aft = (az, rad, lax.rem(ax + n_ax - 1, n_ax))

    barrier = pltpu.get_barrier_semaphore()
    for target in (up, down, partner, fore, aft):
        pl.semaphore_signal(barrier, inc=1, device_id=target, device_id_type=MESH)

    loads = []

    def load(src, dst):
        copy = pltpu.make_async_copy(src, dst, load_sem.at[len(loads)])
        copy.start()
        loads.append(copy)
        return copy

    small = [load(owner, owner_v), load(block, block_v), load(offset, offset_v), load(frac, frac_v), load(count, count_s)]
    bulk = [load(vel, raw.at[0:3, 1 : CA + 1]), load(strain, raw.at[3:9, 1 : CA + 1])]
    tables = [load(lm_avg, own.at[0]), load(mm_avg, own.at[1])]
    later = [load(lm_avg, table.at[0, 0:LINES]), load(mm_avg, table.at[1, 0:LINES])]

    sent = []

    def send(src, dst, target):
        copy = pltpu.make_async_remote_copy(
            src_ref=src, dst_ref=dst, send_sem=send_sem.at[len(sent)], recv_sem=recv_sem.at[len(sent)],
            device_id=target, device_id_type=MESH,
        )
        copy.start()
        sent.append(copy)
        return copy

    halos = []
    lane = lax.broadcasted_iota(jnp.int32, (8, CX), 1)
    for copy in small:
        copy.wait()
    own_id = owner_v[:, 0, :]
    wanted = block_v[:, 0, :]
    self_id = (az * n_rad + rad) * n_ax + ax
    down_id = (down[0] * n_rad + rad) * n_ax + ax
    up_id = (up[0] * n_rad + rad) * n_ax + ax
    rad_id = (az * n_rad + 1 - rad) * n_ax + ax
    line_no = lax.broadcasted_iota(jnp.int32, (CA, CR), 0) * CR + lax.broadcasted_iota(jnp.int32, (CA, CR), 1)
    live = line_no < count_s[self_id]
    hits = [live & (own_id == peer) for peer in (down_id, up_id, rad_id)]
    masks = jnp.concatenate([jnp.where(h, 1.0, 0.0) for h in hits], axis=0)
    row = lax.broadcasted_iota(jnp.int32, (CR, CR), 0)
    col = lax.broadcasted_iota(jnp.int32, (CR, CR), 1)
    prefix = jnp.dot(masks, jnp.where(row <= col, 1.0, 0.0), preferred_element_type=f32)
    totals = jnp.dot(masks, jnp.ones((CR, CR), f32), preferred_element_type=f32)
    row3 = lax.broadcasted_iota(jnp.int32, (3 * CA, 3 * CA), 0)
    col3 = lax.broadcasted_iota(jnp.int32, (3 * CA, 3 * CA), 1)
    before = jnp.where((row3 > col3) & (row3 // CA == col3 // CA), 1.0, 0.0)
    rank = (prefix + jnp.dot(before, totals, preferred_element_type=f32)).astype(jnp.int32) - 1
    slot = jnp.full((CA, CR), -1, jnp.int32)
    place = jnp.where(live, wanted, line_no)
    for k in range(3):
        here = rank[k * CA : (k + 1) * CA] + k * CAP
        slot = jnp.where(hits[k], here, slot)
        place = jnp.where(hits[k], here + LINES, place)
    place_vm[:, 0:CR] = place
    stack[...] = jnp.zeros((CX, CX), f32)
    stack[0:CA, 0:CR] = slot.astype(f32)
    stack[CA : 2 * CA, 0:CR] = wanted.astype(f32)
    stack[2 * CA : 3 * CA, 0:CR] = offset_v[:, 0, :].astype(f32)
    stack[3 * CA : 4 * CA, 0:CR] = frac_v[:, 0, :]
    turned = jnp.transpose(stack[...])[0:CR]
    columns[...] = turned
    slots = lax.broadcasted_iota(jnp.int32, (CR, CX), 1).astype(f32)
    found = [jnp.zeros((CR, CX), f32)] * 3
    for a in range(CA):
        at = jnp.broadcast_to(turned[:, a : a + 1], (CR, CX)) - slots
        number = jnp.broadcast_to(turned[:, CA + a : CA + a + 1], (CR, CX))
        for k in range(3):
            found[k] = jnp.where(at == float(k * CAP), number, found[k])
    for k in range(3):
        ask[k] = jnp.broadcast_to(jnp.sum(found[k], axis=0, keepdims=True), (8, CX)).astype(jnp.int32)
    to_place = pltpu.make_async_copy(place_vm, place_sm, load_sem.at[len(loads)])
    to_place.start()


    for copy in bulk:
        copy.wait()

    @pl.loop(0, CA)
    def pack(a):
        first = last = jnp.zeros((8, CX), f32)
        for g in range(GROUPS):
            for c in range(9):
                at = 9 * g + c
                moved = raw[c, a + 1, 8 * g : 8 * g + 8]
                moved = pltpu.roll(moved, at, 1) if at else moved
                first = jnp.where(lane == at, moved, first)
                last = jnp.where(lane == (at - 1) % CX, moved, last)
        col_send[0, a] = first
        col_send[1, a] = last

    pl.semaphore_wait(barrier, 5)

    queries = [
        send(ask.at[0], asked_vm.at[0], down),
        send(ask.at[1], asked_vm.at[1], up),
        send(ask.at[2], asked_vm.at[2], partner),
    ]
    sides = [
        send(col_send.at[0], cols.at[1, 1 : CA + 1], aft),
        send(col_send.at[1], cols.at[0, 1 : CA + 1], fore),
    ]
    halos += [
        send(vel.at[:, CA - 1], raw.at[0:3, 0], up),
        send(vel.at[:, 0], raw.at[0:3, CA + 1], down),
    ]
    halos += [
        send(strain.at[:, CA - 1], raw.at[3:9, 0], up),
        send(strain.at[:, 0], raw.at[3:9, CA + 1], down),
    ]

    for copy in queries:
        copy.wait()
    to_asked = pltpu.make_async_copy(asked_vm, asked_sm, load_sem.at[len(loads) + 1])
    to_asked.start()
    for copy in tables:
        copy.wait()
    to_asked.wait()

    @pl.loop(0, 3 * (CAP // 64))
    def answer(step):
        k = step // (CAP // 64)
        base = (step % (CAP // 64)) * 64
        for j in range(64):
            number = jnp.clip(asked_sm[k, 0, base + j], 0, LINES - 1)
            for ch in range(2):
                reply[k, ch, pl.ds(base + j, 1)] = own[ch, pl.ds(number, 1)]

    for copy in sides:
        copy.wait()
    corners = [
        send(cols.at[:, CA], cols.at[:, 0], up),
        send(cols.at[:, 1], cols.at[:, CA + 1], down),
    ]
    replies = [
        send(reply.at[0], table.at[:, LINES : LINES + CAP], up),
        send(reply.at[1], table.at[:, LINES + CAP : LINES + 2 * CAP], down),
        send(reply.at[2], table.at[:, LINES + 2 * CAP : LINES + 3 * CAP], partner),
    ]

    keep_aft = jnp.where(ax > 0, 1.0, 0.0)
    keep_fore = jnp.where(ax < n_ax - 1, 1.0, 0.0)
    aft_lane = lax.rem(lane, 9) == 0

    def axial(l, ours):
        low, high = cols[0, l] * keep_aft, cols[1, l] * keep_fore
        ends = []
        for c in range(9):
            low_c = pltpu.roll(low, (1 - c) % CX, 1) if c != 1 else low
            high_c = pltpu.roll(high, CX - 1 - c, 1)
            ends.append(jnp.where(aft_lane, low_c, high_c))
        for g in range(GROUPS):
            rows = slice(8 * g, 8 * g + 8)
            here, behind, ahead = [], [], []
            for c in range(9):
                value = raw[c, l, rows]
                end = pltpu.roll(ends[c], CX - 9 * g, 1) if g else ends[c]
                here.append(value)
                behind.append(jnp.where(lane == 0, end, pltpu.roll(value, 1, 1)))
                ahead.append(jnp.where(lane == CX - 1, end, pltpu.roll(value, CX - 1, 1)))
            here, norm = products(here)
            behind, ahead = products(behind)[0], products(ahead)[0]
            if ours:
                mag[l - 1, rows] = norm
            for ch in range(NCH):
                ax_done[ch, l, rows] = (here[ch] + here[ch]) + (behind[ch] + ahead[ch])

    def azimuthal(ch, layers):
        edges = {}
        for g in range(GROUPS):
            rows = slice(8 * g, 8 * g + 8)
            value = {}
            for l in layers:
                for n in (l - 1, l, l + 1):
                    if n not in value:
                        value[n] = ax_done[ch, n, rows]
                out = (value[l] + value[l]) + (value[l - 1] + value[l + 1])
                az_done[ch, l - 1, 8 * g + 8 : 8 * g + 16] = out
                if g == 0:
                    edges[l] = out[0:1]
                if g == GROUPS - 1:
                    row_send[l - 1, pl.ds(ch, 1)] = jnp.where(rad == 0, out[7:8], edges[l])

    def radial(a):
        for ch in range(NCH):
            value = az_done[ch, a, 8 : CR + 8]
            halo = row_recv[a, ch : ch + 1]
            above = jnp.where(rad == 1, halo, 0.0)
            below = jnp.where(rad == 0, halo, 0.0)
            az_done[ch, a, 7:8] = above
            az_done[ch, a, CR + 8 : CR + 9] = below
            prior = az_done[ch, a, 7 : CR + 7]
            after = az_done[ch, a, 9 : CR + 9]
            rad_done[ch] = ((value + value) + (prior + after)) * (1.0 / 64.0)
        for g in range(GROUPS):
            rows = slice(8 * g, 8 * g + 8)
            lm, mm = contract([rad_done[ch, rows] for ch in range(NCH)])
            lm_here[a, rows] = lm
            mm_here[a, rows] = mm

    pl.loop(1, CA + 1)(lambda l: axial(l, True))
    inner = tuple(range(2, CA))
    pl.loop(0, NCH)(lambda ch: azimuthal(ch, inner))
    rows_in = [send(row_send.at[1 : CA - 1], row_recv.at[1 : CA - 1], partner)]
    rows_in[0].wait()
    pl.loop(1, CA - 1)(radial)

    for copy in halos + corners:
        copy.wait()
    pl.loop(0, 2)(lambda i: axial(i * (CA + 1), False))

    pl.loop(0, NCH)(lambda ch: azimuthal(ch, (1, CA)))
    rows_out = [send(row_send.at[0], row_recv.at[0], partner), send(row_send.at[CA - 1], row_recv.at[CA - 1], partner)]
    for copy in later + replies:
        copy.wait()
    to_place.wait()

    @pl.loop(0, LINES // 64)
    def put(step):
        a = step // (CR // 64)
        base = (step % (CR // 64)) * 64
        for j in range(64):
            number = jnp.clip(place_sm[a, base + j], 0, LINES + 3 * CAP - 1)
            for ch in range(2):
                lines[ch, pl.ds(step * 64 + j, 1)] = table[ch, pl.ds(number, 1)]


    cell = lax.broadcasted_iota(jnp.int32, (CR, CX), 1)
    for a in range(CA):
        shift = jnp.broadcast_to(columns[:, 2 * CA + a : 2 * CA + a + 1], (CR, CX)).astype(jnp.int32)
        weight = jnp.broadcast_to(columns[:, 3 * CA + a : 3 * CA + a + 1], (CR, CX))
        anchor = cell - shift
        left = jnp.maximum(anchor, 0)
        right = jnp.clip(anchor + 1, 0, CX - 1)
        up_lm, up_mm = (
            (1.0 - weight) * jnp.take_along_axis(line, left, axis=1) + weight * jnp.take_along_axis(line, right, axis=1)
            for line in (lines[0, a * CR : (a + 1) * CR], lines[1, a * CR : (a + 1) * CR])
        )
        theta = 0.5 * jnp.sqrt(jnp.sqrt(jnp.sqrt(jnp.maximum(up_lm, 0.0) * up_mm)))
        eps = theta / (1.0 + theta)
        upstream[0, a] = eps
        upstream[1, a] = (1.0 - eps) * up_lm
        upstream[2, a] = (1.0 - eps) * up_mm

    for copy in rows_out:
        copy.wait()

    @pl.loop(0, 2)
    def edge_radial(i):
        radial(i * (CA - 1))

def relax_kernel(upstream, lm_here, mm_here, mag, lm_new, mm_new, eddy):
    for a in range(CA):
        eps = upstream[0, a]
        lm = jnp.maximum(eps * lm_here[a] + upstream[1, a], 0.0)
        mm = eps * mm_here[a] + upstream[2, a]
        lm_new[a] = lm
        mm_new[a] = mm
        eddy[a] = 0.25 * lm / mm * mag[a]


def on_device(velocity, strain_rate, lm_average, mm_average, source_owner, source_block, offset_cells, fraction, query_count):
    grid = (CA, CR, CX)
    line_form = (LINES, CX)
    flat = (CA, 1, CR)
    SDS = jax.ShapeDtypeStruct
    VMEM = pltpu.VMEM
    whole = pl.BlockSpec(memory_space=pltpu.VMEM)
    upstream, lm_here, mm_here, mag = pl.pallas_call(
        exchange_kernel,
        out_shape=[VMEM((3,) + grid, f32), VMEM(grid, f32), VMEM(grid, f32), VMEM(grid, f32)],
        in_specs=[pl.BlockSpec(memory_space=pltpu.HBM)] * 9,
        out_specs=[whole] * 4,
        scratch_shapes=[
            VMEM((2,) + line_form, f32),
            VMEM((CR, CX), f32),
            VMEM((9, CA + 2, CR, CX), f32),
            VMEM((2, CA + 2, 8, CX), f32),
            VMEM((2, CA, 8, CX), f32),
            VMEM((NCH, CA + 2, CR, CX), f32),
            VMEM((NCH, CA, CR + 16, CX), f32),
            VMEM((CA, 24, CX), f32),
            VMEM((CA, 24, CX), f32),
            VMEM((NCH, CR, CX), f32),
            VMEM((2,) + line_form, f32),
            VMEM((2, LINES + 3 * CAP, CX), f32),
            VMEM((3, 2, CAP, CX), f32),
            VMEM((3, 8, CX), jnp.int32),
            VMEM((3, 8, CX), jnp.int32),
            pltpu.SMEM((3, 8, CX), jnp.int32),
            VMEM((CA, CX), jnp.int32),
            pltpu.SMEM((CA, CX), jnp.int32),
            VMEM(flat, jnp.int32),
            VMEM(flat, jnp.int32),
            VMEM(flat, jnp.int32),
            VMEM(flat, f32),
            pltpu.SMEM(query_count.shape, jnp.int32),
            VMEM((CX, CX), f32),
            pltpu.SemaphoreType.DMA((16,)),
            pltpu.SemaphoreType.DMA((20,)),
            pltpu.SemaphoreType.DMA((20,)),
        ],
        compiler_params=pltpu.CompilerParams(collective_id=0, has_side_effects=True, vmem_limit_bytes=VMEM_LIMIT),
        name="exchange",
    )(*(pltpu.with_memory_space_constraint(x, pltpu.HBM) for x in (
        velocity, strain_rate, lm_average.reshape(line_form), mm_average.reshape(line_form),
        source_owner.reshape(flat), source_block.reshape(flat), offset_cells.reshape(flat), fraction.reshape(flat),
        query_count,
    )))
    return pl.pallas_call(
        relax_kernel,
        out_shape=[SDS(grid, f32)] * 3,
        in_specs=[whole] * 4,
        out_specs=[whole] * 3,
        compiler_params=pltpu.CompilerParams(vmem_limit_bytes=32 * 2**20),
        name="relax",
    )(upstream, lm_here, mm_here, mag)


def solution(mesh):
    cells, lines = P(None, "az", "rad", "ax"), P("az", "rad", "ax")
    return jax.shard_map(
        on_device,
        mesh=mesh,
        in_specs=(cells, cells) + (lines,) * 6 + (P(),),
        out_specs=(lines, lines, lines),
        check_vma=False,
    )
```

```python
import jax
import jax.numpy as jnp
from jax import lax
from jax.experimental import pallas as pl
from jax.experimental.pallas import tpu as pltpu
from jax.sharding import PartitionSpec as P

MESH = pl.DeviceIdType.MESH
pair_list = ((0, 0), (1, 1), (2, 2), (0, 1), (0, 2), (1, 2))
CA, CR, CX = 8, 64, 128
NCH = 21
LINES = CA * CR
CAP = LINES // 4
GROUPS = CR // 8
f32 = jnp.float32
VMEM_LIMIT = 48000 * 2**10


def strain_norm(s):
    normal = s[0] * s[0] + s[1] * s[1] + s[2] * s[2]
    shearing = s[3] * s[3] + s[4] * s[4] + s[5] * s[5]
    return jnp.sqrt(2.0 * normal + 4.0 * shearing)


def products(raw):
    vel, strain = raw[:3], raw[3:]
    magnitude = strain_norm(strain)
    fields = list(vel)
    fields += [vel[i] * vel[j] for i, j in pair_list]
    fields += strain
    fields += [magnitude * s for s in strain]
    return fields, magnitude


def contract(filtered):
    strain = [filtered[9 + c] for c in range(6)]
    four_norm = 4.0 * strain_norm(strain)
    sums = []
    for channels in ((0, 1, 2), (3, 4, 5)):
        lm = mm = None
        for c in channels:
            i, j = pair_list[c]
            leonard = filtered[3 + c] - filtered[i] * filtered[j]
            model = filtered[15 + c] - four_norm * strain[c]
            lm = leonard * model if lm is None else lm + leonard * model
            mm = model * model if mm is None else mm + model * model
        sums.append((lm, mm))
    (lm_a, mm_a), (lm_b, mm_b) = sums
    return 0.5 * lm_a + lm_b, 0.25 * mm_a + 0.5 * mm_b


def exchange_kernel(
    vel, strain, lm_avg, mm_avg, owner, block, offset, frac, count,
    upstream, lm_here, mm_here, mag,
    lines, columns,
    raw, cols, col_send, ax_done, az_done, row_send, row_recv, rad_done,
    own, table, reply, ask, asked_vm, asked_sm, place_vm, place_sm,
    owner_v, block_v, offset_v, frac_v, count_s, stack,
    load_sem, send_sem, recv_sem,
):
    az, rad, ax = lax.axis_index("az"), lax.axis_index("rad"), lax.axis_index("ax")
    n_az, n_rad, n_ax = lax.axis_size("az"), lax.axis_size("rad"), lax.axis_size("ax")
    up = (lax.rem(az + 1, n_az), rad, ax)
    down = (lax.rem(az + n_az - 1, n_az), rad, ax)
    partner = (az, 1 - rad, ax)
    fore = (az, rad, lax.rem(ax + 1, n_ax))
    aft = (az, rad, lax.rem(ax + n_ax - 1, n_ax))

    barrier = pltpu.get_barrier_semaphore()
    for target in (up, down, partner, fore, aft):
        pl.semaphore_signal(barrier, inc=1, device_id=target, device_id_type=MESH)

    loads = []

    def load(src, dst):
        copy = pltpu.make_async_copy(src, dst, load_sem.at[len(loads)])
        copy.start()
        loads.append(copy)
        return copy

    small = [load(owner, owner_v), load(block, block_v), load(offset, offset_v), load(frac, frac_v), load(count, count_s)]
    bulk = [load(vel, raw.at[0:3, 1 : CA + 1]), load(strain, raw.at[3:9, 1 : CA + 1])]
    tables = [load(lm_avg, own.at[0]), load(mm_avg, own.at[1])]
    later = [load(lm_avg, table.at[0, 0:LINES]), load(mm_avg, table.at[1, 0:LINES])]

    sent = []

    def send(src, dst, target):
        copy = pltpu.make_async_remote_copy(
            src_ref=src, dst_ref=dst, send_sem=send_sem.at[len(sent)], recv_sem=recv_sem.at[len(sent)],
            device_id=target, device_id_type=MESH,
        )
        copy.start()
        sent.append(copy)
        return copy

    halos = []
    lane = lax.broadcasted_iota(jnp.int32, (8, CX), 1)
    for copy in small:
        copy.wait()
    own_id = owner_v[:, 0, :]
    wanted = block_v[:, 0, :]
    self_id = (az * n_rad + rad) * n_ax + ax
    down_id = (down[0] * n_rad + rad) * n_ax + ax
    up_id = (up[0] * n_rad + rad) * n_ax + ax
    rad_id = (az * n_rad + 1 - rad) * n_ax + ax
    line_no = lax.broadcasted_iota(jnp.int32, (CA, CR), 0) * CR + lax.broadcasted_iota(jnp.int32, (CA, CR), 1)
    live = line_no < count_s[self_id]
    hits = [live & (own_id == peer) for peer in (down_id, up_id, rad_id)]
    masks = jnp.concatenate([jnp.where(h, 1.0, 0.0) for h in hits], axis=0)
    row = lax.broadcasted_iota(jnp.int32, (CR, CR), 0)
    col = lax.broadcasted_iota(jnp.int32, (CR, CR), 1)
    prefix = jnp.dot(masks, jnp.where(row <= col, 1.0, 0.0), preferred_element_type=f32)
    totals = jnp.dot(masks, jnp.ones((CR, CR), f32), preferred_element_type=f32)
    row3 = lax.broadcasted_iota(jnp.int32, (3 * CA, 3 * CA), 0)
    col3 = lax.broadcasted_iota(jnp.int32, (3 * CA, 3 * CA), 1)
    before = jnp.where((row3 > col3) & (row3 // CA == col3 // CA), 1.0, 0.0)
    rank = (prefix + jnp.dot(before, totals, preferred_element_type=f32)).astype(jnp.int32) - 1
    slot = jnp.full((CA, CR), -1, jnp.int32)
    place = jnp.where(live, wanted, line_no)
    for k in range(3):
        here = rank[k * CA : (k + 1) * CA] + k * CAP
        slot = jnp.where(hits[k], here, slot)
        place = jnp.where(hits[k], here + LINES, place)
    place_vm[:, 0:CR] = place
    stack[...] = jnp.zeros((CX, CX), f32)
    stack[0:CA, 0:CR] = slot.astype(f32)
    stack[CA : 2 * CA, 0:CR] = wanted.astype(f32)
    stack[2 * CA : 3 * CA, 0:CR] = offset_v[:, 0, :].astype(f32)
    stack[3 * CA : 4 * CA, 0:CR] = frac_v[:, 0, :]
    turned = jnp.transpose(stack[...])[0:CR]
    columns[...] = turned
    slots = lax.broadcasted_iota(jnp.int32, (CR, CX), 1).astype(f32)
    found = [jnp.zeros((CR, CX), f32)] * 3
    for a in range(CA):
        at = jnp.broadcast_to(turned[:, a : a + 1], (CR, CX)) - slots
        number = jnp.broadcast_to(turned[:, CA + a : CA + a + 1], (CR, CX))
        for k in range(3):
            found[k] = jnp.where(at == float(k * CAP), number, found[k])
    for k in range(3):
        ask[k] = jnp.broadcast_to(jnp.sum(found[k], axis=0, keepdims=True), (8, CX)).astype(jnp.int32)
    to_place = pltpu.make_async_copy(place_vm, place_sm, load_sem.at[len(loads)])
    to_place.start()


    for copy in bulk:
        copy.wait()

    @pl.loop(0, CA)
    def pack(a):
        first = last = jnp.zeros((8, CX), f32)
        for g in range(GROUPS):
            for c in range(9):
                at = 9 * g + c
                moved = raw[c, a + 1, 8 * g : 8 * g + 8]
                moved = pltpu.roll(moved, at, 1) if at else moved
                first = jnp.where(lane == at, moved, first)
                last = jnp.where(lane == (at - 1) % CX, moved, last)
        col_send[0, a] = first
        col_send[1, a] = last

    pl.semaphore_wait(barrier, 5)

    queries = [
        send(ask.at[0], asked_vm.at[0], down),
        send(ask.at[1], asked_vm.at[1], up),
        send(ask.at[2], asked_vm.at[2], partner),
    ]
    sides = [
        send(col_send.at[0], cols.at[1, 1 : CA + 1], aft),
        send(col_send.at[1], cols.at[0, 1 : CA + 1], fore),
    ]
    halos += [
        send(vel.at[:, CA - 1], raw.at[0:3, 0], up),
        send(vel.at[:, 0], raw.at[0:3, CA + 1], down),
    ]
    halos += [
        send(strain.at[:, CA - 1], raw.at[3:9, 0], up),
        send(strain.at[:, 0], raw.at[3:9, CA + 1], down),
    ]

    for copy in queries:
        copy.wait()
    to_asked = pltpu.make_async_copy(asked_vm, asked_sm, load_sem.at[len(loads) + 1])
    to_asked.start()
    for copy in tables:
        copy.wait()
    to_asked.wait()

    def answer(k):
        @pl.loop(0, CAP // 64)
        def lines_of(step):
            base = step * 64
            for j in range(64):
                number = jnp.clip(asked_sm[k, 0, base + j], 0, LINES - 1)
                for ch in range(2):
                    reply[k, ch, pl.ds(base + j, 1)] = own[ch, pl.ds(number, 1)]

    answer(0)
    for copy in sides:
        copy.wait()
    corners = [
        send(cols.at[:, CA], cols.at[:, 0], up),
        send(cols.at[:, 1], cols.at[:, CA + 1], down),
    ]
    replies = []
    for k, target in enumerate((up, down, partner)):
        if k:
            answer(k)
        first = LINES + k * CAP
        replies.append(send(reply.at[k], table.at[:, first : first + CAP], target))

    keep_aft = jnp.where(ax > 0, 1.0, 0.0)
    keep_fore = jnp.where(ax < n_ax - 1, 1.0, 0.0)
    aft_lane = lax.rem(lane, 9) == 0

    def axial(l, ours):
        low, high = cols[0, l] * keep_aft, cols[1, l] * keep_fore
        ends = []
        for c in range(9):
            low_c = pltpu.roll(low, (1 - c) % CX, 1) if c != 1 else low
            high_c = pltpu.roll(high, CX - 1 - c, 1)
            ends.append(jnp.where(aft_lane, low_c, high_c))
        for g in range(GROUPS):
            rows = slice(8 * g, 8 * g + 8)
            here, behind, ahead = [], [], []
            for c in range(9):
                value = raw[c, l, rows]
                end = pltpu.roll(ends[c], CX - 9 * g, 1) if g else ends[c]
                here.append(value)
                behind.append(jnp.where(lane == 0, end, pltpu.roll(value, 1, 1)))
                ahead.append(jnp.where(lane == CX - 1, end, pltpu.roll(value, CX - 1, 1)))
            here, norm = products(here)
            behind, ahead = products(behind)[0], products(ahead)[0]
            if ours:
                mag[l - 1, rows] = norm
            for ch in range(NCH):
                ax_done[ch, l, rows] = (here[ch] + here[ch]) + (behind[ch] + ahead[ch])

    def azimuthal(ch, layers):
        edges = {}
        for g in range(GROUPS):
            rows = slice(8 * g, 8 * g + 8)
            value = {}
            for l in layers:
                for n in (l - 1, l, l + 1):
                    if n not in value:
                        value[n] = ax_done[ch, n, rows]
                out = (value[l] + value[l]) + (value[l - 1] + value[l + 1])
                az_done[ch, l - 1, 8 * g + 8 : 8 * g + 16] = out
                if g == 0:
                    edges[l] = out[0:1]
                if g == GROUPS - 1:
                    row_send[l - 1, pl.ds(ch, 1)] = jnp.where(rad == 0, out[7:8], edges[l])

    def radial(a):
        for ch in range(NCH):
            value = az_done[ch, a, 8 : CR + 8]
            halo = row_recv[a, ch : ch + 1]
            above = jnp.where(rad == 1, halo, 0.0)
            below = jnp.where(rad == 0, halo, 0.0)
            az_done[ch, a, 7:8] = above
            az_done[ch, a, CR + 8 : CR + 9] = below
            prior = az_done[ch, a, 7 : CR + 7]
            after = az_done[ch, a, 9 : CR + 9]
            rad_done[ch] = ((value + value) + (prior + after)) * (1.0 / 64.0)
        for g in range(GROUPS):
            rows = slice(8 * g, 8 * g + 8)
            lm, mm = contract([rad_done[ch, rows] for ch in range(NCH)])
            lm_here[a, rows] = lm
            mm_here[a, rows] = mm

    pl.loop(1, CA + 1)(lambda l: axial(l, True))
    inner = tuple(range(2, CA))
    pl.loop(0, NCH)(lambda ch: azimuthal(ch, inner))
    rows_in = [send(row_send.at[1 : CA - 1], row_recv.at[1 : CA - 1], partner)]
    rows_in[0].wait()
    pl.loop(1, CA - 1)(radial)

    for copy in halos + corners:
        copy.wait()
    pl.loop(0, 2)(lambda i: axial(i * (CA + 1), False))

    pl.loop(0, NCH)(lambda ch: azimuthal(ch, (1, CA)))
    rows_out = [send(row_send.at[0], row_recv.at[0], partner), send(row_send.at[CA - 1], row_recv.at[CA - 1], partner)]
    for copy in later + replies:
        copy.wait()
    to_place.wait()

    @pl.loop(0, LINES // 64)
    def put(step):
        a = step // (CR // 64)
        base = (step % (CR // 64)) * 64
        for j in range(64):
            number = jnp.clip(place_sm[a, base + j], 0, LINES + 3 * CAP - 1)
            for ch in range(2):
                lines[ch, pl.ds(step * 64 + j, 1)] = table[ch, pl.ds(number, 1)]


    cell = lax.broadcasted_iota(jnp.int32, (CR, CX), 1)
    for a in range(CA):
        shift = jnp.broadcast_to(columns[:, 2 * CA + a : 2 * CA + a + 1], (CR, CX)).astype(jnp.int32)
        weight = jnp.broadcast_to(columns[:, 3 * CA + a : 3 * CA + a + 1], (CR, CX))
        anchor = cell - shift
        left = jnp.maximum(anchor, 0)
        right = jnp.clip(anchor + 1, 0, CX - 1)
        up_lm, up_mm = (
            (1.0 - weight) * jnp.take_along_axis(line, left, axis=1) + weight * jnp.take_along_axis(line, right, axis=1)
            for line in (lines[0, a * CR : (a + 1) * CR], lines[1, a * CR : (a + 1) * CR])
        )
        theta = 0.5 * jnp.sqrt(jnp.sqrt(jnp.sqrt(jnp.maximum(up_lm, 0.0) * up_mm)))
        eps = theta / (1.0 + theta)
        upstream[0, a] = eps
        upstream[1, a] = (1.0 - eps) * up_lm
        upstream[2, a] = (1.0 - eps) * up_mm

    for copy in rows_out:
        copy.wait()

    @pl.loop(0, 2)
    def edge_radial(i):
        radial(i * (CA - 1))

def relax_kernel(upstream, lm_here, mm_here, mag, lm_new, mm_new, eddy):
    for a in range(CA):
        eps = upstream[0, a]
        lm = jnp.maximum(eps * lm_here[a] + upstream[1, a], 0.0)
        mm = eps * mm_here[a] + upstream[2, a]
        lm_new[a] = lm
        mm_new[a] = mm
        eddy[a] = 0.25 * lm / mm * mag[a]


def on_device(velocity, strain_rate, lm_average, mm_average, source_owner, source_block, offset_cells, fraction, query_count):
    grid = (CA, CR, CX)
    line_form = (LINES, CX)
    flat = (CA, 1, CR)
    SDS = jax.ShapeDtypeStruct
    VMEM = pltpu.VMEM
    whole = pl.BlockSpec(memory_space=pltpu.VMEM)
    upstream, lm_here, mm_here, mag = pl.pallas_call(
        exchange_kernel,
        out_shape=[VMEM((3,) + grid, f32), VMEM(grid, f32), VMEM(grid, f32), VMEM(grid, f32)],
        in_specs=[pl.BlockSpec(memory_space=pltpu.HBM)] * 9,
        out_specs=[whole] * 4,
        scratch_shapes=[
            VMEM((2,) + line_form, f32),
            VMEM((CR, CX), f32),
            VMEM((9, CA + 2, CR, CX), f32),
            VMEM((2, CA + 2, 8, CX), f32),
            VMEM((2, CA, 8, CX), f32),
            VMEM((NCH, CA + 2, CR, CX), f32),
            VMEM((NCH, CA, CR + 16, CX), f32),
            VMEM((CA, 24, CX), f32),
            VMEM((CA, 24, CX), f32),
            VMEM((NCH, CR, CX), f32),
            VMEM((2,) + line_form, f32),
            VMEM((2, LINES + 3 * CAP, CX), f32),
            VMEM((3, 2, CAP, CX), f32),
            VMEM((3, 8, CX), jnp.int32),
            VMEM((3, 8, CX), jnp.int32),
            pltpu.SMEM((3, 8, CX), jnp.int32),
            VMEM((CA, CX), jnp.int32),
            pltpu.SMEM((CA, CX), jnp.int32),
            VMEM(flat, jnp.int32),
            VMEM(flat, jnp.int32),
            VMEM(flat, jnp.int32),
            VMEM(flat, f32),
            pltpu.SMEM(query_count.shape, jnp.int32),
            VMEM((CX, CX), f32),
            pltpu.SemaphoreType.DMA((16,)),
            pltpu.SemaphoreType.DMA((20,)),
            pltpu.SemaphoreType.DMA((20,)),
        ],
        compiler_params=pltpu.CompilerParams(collective_id=0, has_side_effects=True, vmem_limit_bytes=VMEM_LIMIT),
        name="exchange",
    )(*(pltpu.with_memory_space_constraint(x, pltpu.HBM) for x in (
        velocity, strain_rate, lm_average.reshape(line_form), mm_average.reshape(line_form),
        source_owner.reshape(flat), source_block.reshape(flat), offset_cells.reshape(flat), fraction.reshape(flat),
        query_count,
    )))
    return pl.pallas_call(
        relax_kernel,
        out_shape=[SDS(grid, f32)] * 3,
        in_specs=[whole] * 4,
        out_specs=[whole] * 3,
        compiler_params=pltpu.CompilerParams(vmem_limit_bytes=32 * 2**20),
        name="relax",
    )(upstream, lm_here, mm_here, mag)


def solution(mesh):
    cells, lines = P(None, "az", "rad", "ax"), P("az", "rad", "ax")
    return jax.shard_map(
        on_device,
        mesh=mesh,
        in_specs=(cells, cells) + (lines,) * 6 + (P(),),
        out_specs=(lines, lines, lines),
        check_vma=False,
    )
```
